32 devices in a mesh: queue: 16 (over z, x, core), mp: 2 (over y).
Axes of the slice: x: 2, y: 2, z: 4, core: 2. Of those that a mesh axis runs over, the one named last changes fastest.
Arguments:
- speech: bfloat16 [3072, 1024], P(('queue', 'mp')), may hold values from -6 to 6
- weight: bfloat16 [1024, 1024], P(None, 'mp'), may hold values from -0.1875 to 0.1875
- norm_gain: float32 [1024], replicated, may hold values from 0.1 to 1.9
- queue_keys: bfloat16 [12288, 1024], P('queue'), may hold values from -96 to 96
- new_keys: bfloat16 [768, 1024], replicated, may hold values from -6 to 6
- pointer: int32 [1], replicated, may hold values from 0 to 12287
- positives: int32 [3072], P(('queue', 'mp')), may hold values from 0 to 12287
Outputs:
- loss: float32 [3072], P(('queue', 'mp'))
- grad_speech: bfloat16 [3072, 1024], P(('queue', 'mp'))
- queue_next: bfloat16 [12288, 1024], P('queue')
The draws below stay inside these ranges and needn't reach their ends.
All inputs are finite; a program needn't handle non-finite values.
Results may differ from the reference program's by a relative error of at most 0.022.
The reference program's roundings to bfloat16 on the way (of `queries`, `weights` and `hidden_grad`) count: a program that leaves them out, or rounds other values in their place, can miss the bound.
Values may be sent and summed in bfloat16 or wider, within the bound.
A program may use at most 128 MiB of HBM per device.

```python
import math
import jax
import jax.numpy as jnp
from jax import lax

D = 1024
KEY_DEV = 768
QUERIES = 3072
QUEUE = 12288
N_QUEUE = 16


def draw_queue_keys(key, part):
    key = jax.random.fold_in(key, 7)
    entry_key = jax.random.fold_in(key, 0)
    values = jax.random.normal(entry_key, (QUEUE, D), jnp.float32)
    return values.astype(jnp.bfloat16)


def touch_ends(array, stream_key, smallest, top_value):
    extent = array.shape
    spot = [jax.random.randint(jax.random.fold_in(stream_key, axis), (), 0, extent[axis]) for axis in range(len(extent))]
    array = array.at[tuple(spot)].set(smallest)
    longest = extent.index(max(extent))
    spot[longest] = (spot[longest] + 1) % extent[longest]
    return array.at[tuple(spot)].set(top_value)


def level_of(key, shape, cuts, least, high):
    def one(position, parts):
        heights = jax.random.uniform(jax.random.fold_in(jax.random.fold_in(key, 6), position), (parts,), jnp.float32, least / len(cuts), high / len(cuts))
        return jnp.repeat(jnp.exp(heights), shape[position] // parts).reshape((-1,) + (1,) * (len(shape) - position - 1))

    loudness = one(*cuts[0])
    for cut in cuts[1:]:
        loudness = loudness * one(*cut)
    return loudness


def gaussian(stream_key, shape, spread, limit, cuts=(), held_as=jnp.bfloat16):
    result = spread * jax.random.normal(stream_key, shape, jnp.float32)
    if cuts:
        result = result * level_of(stream_key, shape, cuts, -0.22, 0.18)
    return jnp.clip(result, -limit, limit).astype(held_as)


def setup_inputs(seed: int = 0) -> dict:
    seeds = jax.random.split(jax.random.key(seed), 8)
    speech = gaussian(seeds[0], (QUERIES, D), 1.0, 6.0, ((0, 32),))
    weight = gaussian(seeds[1], (D, D), D ** -0.5, 0.1875, ((1, 2),))
    norm_gain = jnp.clip(1.0 + 0.18 * jax.random.normal(seeds[2], (D,), jnp.float32), 0.1, 1.9)
    queue_keys = draw_queue_keys(jax.random.fold_in(seeds[7], 71), 0)
    new_keys = gaussian(seeds[4], (KEY_DEV, D), 1.0, 6.0)
    pointer = jax.random.randint(seeds[5], (1,), 0, QUEUE).astype(jnp.int32)
    positives = touch_ends(jax.random.randint(seeds[6], (QUERIES,), 0, QUEUE), jax.random.fold_in(seeds[6], 1), 0, QUEUE - 1).astype(jnp.int32)
    return dict(speech=speech, weight=weight, norm_gain=norm_gain, queue_keys=queue_keys, new_keys=new_keys, pointer=pointer, positives=positives)


def reference(speech, weight, norm_gain, queue_keys, new_keys, pointer, positives):
    hidden = jnp.dot(speech, weight, preferred_element_type=jnp.float32)
    inverse_rms = lax.rsqrt(lax.optimization_barrier(jnp.mean(hidden * hidden, axis=1, keepdims=True)) + 1e-06)
    queries = (hidden * inverse_rms * norm_gain).astype(jnp.bfloat16)
    factor = 2.0 / math.sqrt(D)
    blocks = queue_keys.reshape(N_QUEUE, KEY_DEV, D)
    block_ids = jnp.arange(N_QUEUE, dtype=jnp.int32)
    column_ids = jnp.arange(KEY_DEV, dtype=jnp.int32)

    def block_scores(key_rows, block_id):
        scores = lax.dot_general(queries, key_rows, (((1,), (1,)), ((), ())), preferred_element_type=jnp.float32) * factor
        is_positive = column_ids[None, :] == (positives - block_id * KEY_DEV)[:, None]
        return (scores, is_positive)

    def forward(carry, pieces):
        row_peak, row_total, row_positive = carry
        scores, is_positive = block_scores(pieces[0], pieces[1])
        new_peak = jnp.maximum(row_peak, lax.optimization_barrier(jnp.max(scores, axis=1)))
        row_total = row_total * jnp.exp(row_peak - new_peak) + lax.optimization_barrier(jnp.sum(jnp.exp(scores - new_peak[:, None]), axis=1))
        row_positive = row_positive + lax.optimization_barrier(jnp.sum(jnp.where(is_positive, scores, 0.0), axis=1))
        return ((new_peak, row_total, row_positive), None)
    start_state = (jnp.full((QUERIES,), -1e+30, jnp.float32), jnp.zeros((QUERIES,), jnp.float32), jnp.zeros((QUERIES,), jnp.float32))
    (row_peak, row_total, row_positive), _ = lax.scan(forward, start_state, (blocks, block_ids))
    log_total = row_peak + jnp.log(row_total)
    loss = log_total - row_positive

    def backward(carry, pieces):
        scores, is_positive = block_scores(pieces[0], pieces[1])
        weights = (jnp.exp(scores - log_total[:, None]) - is_positive.astype(jnp.float32)).astype(jnp.bfloat16)
        partial_grad = jnp.dot(weights, pieces[0], preferred_element_type=jnp.float32).astype(jnp.bfloat16)
        partial_grad = lax.optimization_barrier(partial_grad)
        return (carry + partial_grad.astype(jnp.float32), None)
    summed, _ = lax.scan(backward, jnp.zeros((QUERIES, D), jnp.float32), (blocks, block_ids))
    key_grad = summed * (16.0 * factor)
    scaled = norm_gain * key_grad
    cubed = inverse_rms * inverse_rms * inverse_rms
    hidden_grad = (inverse_rms * scaled - hidden * cubed * lax.optimization_barrier(jnp.sum(scaled * hidden, axis=1, keepdims=True)) / D).astype(jnp.bfloat16)
    grad_speech = lax.dot_general(hidden_grad, weight, (((1,), (1,)), ((), ())), preferred_element_type=jnp.float32).astype(jnp.bfloat16)
    row_ids = jnp.arange(QUEUE, dtype=jnp.int32)
    offsets = ((row_ids - pointer[0]) % QUEUE).astype(jnp.int32)
    replaced = offsets < KEY_DEV
    taken = jnp.take(new_keys, jnp.minimum(offsets, KEY_DEV - 1).astype(jnp.int32), axis=0)
    queue_next = jnp.where(replaced[:, None], taken, queue_keys)
    return (loss, grad_speech, queue_next)
```

```python
import functools
import math

import jax
import jax.numpy as jnp
from jax import lax
from jax.experimental import pallas as pl
from jax.experimental.pallas import tpu as pltpu
from jax.sharding import PartitionSpec as P

MESH = pl.DeviceIdType.MESH
GROUP = 4
WEIGHT_CHUNKS = 4
KEY_CHUNKS = 6
LANES = 128


def column_of(tile, row, count):
    line = jnp.broadcast_to(tile[row : row + 1, :], (LANES, LANES))
    eye = lax.broadcasted_iota(jnp.int32, (LANES, LANES), 0) == lax.broadcasted_iota(
        jnp.int32, (LANES, LANES), 1
    )
    return jnp.sum(jnp.where(eye, line, jnp.zeros_like(line)), axis=1, keepdims=True)[:count]


def row_of(column):
    count = column.shape[0]
    wide = jnp.broadcast_to(column, (count, LANES))
    eye = lax.broadcasted_iota(jnp.int32, (count, LANES), 0) == lax.broadcasted_iota(
        jnp.int32, (count, LANES), 1
    )
    return jnp.sum(jnp.where(eye, wide, jnp.zeros_like(wide)), axis=0, keepdims=True)


def step_kernel(
    n_queue,
    n_mp,
    speech_ref,
    weight_ref,
    gain_ref,
    keys_ref,
    new_ref,
    pointer_ref,
    positives_ref,
    loss_ref,
    grad_ref,
    next_ref,
    keys,
    weights_in,
    queries,
    columns,
    scores,
    probs,
    hidden,
    partial,
    arrived,
    stats,
    local_sem,
    wy_s, wy_r, wx_s, wx_r, wcy_s, wcy_r, wcx_s, wcx_r, wco_s, wco_r,
    kc_s, kc_r, kx_s, kx_r, ky_s, ky_r, kcx_s, kcx_r, kcy_s, kcy_r,
    q_s, q_r, p_s, p_r, st_s, st_r, g_s, g_r,
):
    rows, width = speech_ref.shape
    key_count = keys_ref.shape[0]
    nz = n_queue // GROUP
    me = lax.axis_index("queue")
    mp = lax.axis_index("mp")
    z = me // GROUP
    slot = me % GROUP
    x = slot // 2
    core = slot % 2
    core_peer = me + 1 - 2 * core
    x_peer = me + 2 - 4 * x
    core_slot = slot + 1 - 2 * core
    x_slot = slot + 2 - 4 * x
    diag_slot = core_slot + 2 - 4 * x

    def z_dev(distance):
        return lax.rem(z + distance, nz) * GROUP + slot

    def mp_dev(distance):
        return lax.rem(mp + distance, n_mp)

    def push(src, dst, send, recv, queue, mp_index):
        return pltpu.make_async_remote_copy(
            src_ref=src, dst_ref=dst, send_sem=send, recv_sem=recv,
            device_id=(queue, mp_index), device_id_type=MESH,
        )

    barrier = pltpu.get_barrier_semaphore()
    peers = [(core_peer, mp), (x_peer, mp)]
    peers += [(me, mp_dev(d)) for d in range(1, n_mp)]
    peers += [(z_dev(d), mp) for d in range(1, nz)]
    for peer in peers:
        pl.semaphore_signal(barrier, inc=1, device_id=peer, device_id_type=MESH)

    def key_rows(which, start, count):
        return keys.at[pl.ds(pl.multiple_of(which * key_count + start, 16), count), :]

    own_keys = pltpu.make_async_copy(keys_ref, key_rows(slot, 0, key_count), local_sem.at[0])
    own_weight = pltpu.make_async_copy(weight_ref, weights_in.at[mp], local_sem.at[1])
    own_keys.start()
    own_weight.start()
    pl.semaphore_wait(barrier, len(peers))

    sends = []

    def start(copy):
        copy.start()
        sends.append(copy)

    w_count = width // GROUP // WEIGHT_CHUNKS

    def w_push(dist, quarter, j, shard, sems, queue, mp_index, src=None):
        at = pl.ds(pl.multiple_of(quarter * (width // GROUP) + j * w_count, 16), w_count)
        dst = weights_in.at[shard, at, :]
        return push(
            dst if src is None else src.at[at, :], dst,
            sems[0].at[dist, j], sems[1].at[dist, j], queue, mp_index,
        )

    for j in range(WEIGHT_CHUNKS):
        for d in range(1, n_mp):
            start(w_push(d, slot, j, mp, (wy_s, wy_r), me, mp_dev(d), weight_ref))

    part = key_count // n_mp
    k_count = part // KEY_CHUNKS

    def k_start(shard, j):
        return shard * part + j * k_count

    def key_x(j):
        at = k_start(mp, j)
        return push(
            keys_ref.at[pl.ds(pl.multiple_of(at, 16), k_count), :], key_rows(slot, at, k_count),
            kx_s.at[j], kx_r.at[j], x_peer, mp,
        )

    start(key_x(0))
    start(push(keys_ref, key_rows(slot, 0, key_count), kc_s.at[0], kc_r.at[0], core_peer, mp))

    for j in range(WEIGHT_CHUNKS):
        for d in range(1, n_mp):
            shard = mp_dev(n_mp - d)
            w_push(d, slot, j, shard, (wy_s, wy_r), me, mp).wait_recv()
            start(w_push(d, slot, j, shard, (wx_s, wx_r), x_peer, mp))
            start(w_push(d, slot, j, shard, (wcy_s, wcy_r), core_peer, mp))
    for j in range(1, KEY_CHUNKS):
        start(key_x(j))
    for j in range(WEIGHT_CHUNKS):
        for d in range(1, n_mp):
            shard = mp_dev(n_mp - d)
            w_push(d, x_slot, j, shard, (wx_s, wx_r), x_peer, mp).wait_recv()
            start(w_push(d, x_slot, j, shard, (wcx_s, wcx_r), core_peer, mp))
    own_weight.wait()
    for j in range(WEIGHT_CHUNKS):
        for d in range(1, n_mp):
            shard = mp_dev(n_mp - d)
            w_push(d, core_slot, j, shard, (wcy_s, wcy_r), core_peer, mp).wait_recv()
            w_push(d, diag_slot, j, shard, (wcx_s, wcx_r), core_peer, mp).wait_recv()

    part_width = width // n_mp
    for m in range(n_mp):
        hidden[:, m * part_width : (m + 1) * part_width] = jnp.dot(
            speech_ref[...], weights_in[m], preferred_element_type=jnp.float32
        )
    encoded = hidden[...]
    inverse_rms = lax.rsqrt(jnp.mean(encoded * encoded, axis=1, keepdims=True) + 1e-06)
    own_rows = pl.ds(pl.multiple_of(z * rows, 16), rows)
    queries[own_rows, :] = (encoded * inverse_rms * gain_ref[...]).astype(jnp.bfloat16)
    columns[z] = positives_ref[...]

    def z_rows(index):
        return pl.ds(pl.multiple_of(index * rows, 16), rows)

    def query_push(d, owner, target):
        at = queries.at[z_rows(owner), :]
        return push(at, at, q_s.at[d], q_r.at[d], target, mp)

    def column_push(d, owner, target):
        at = columns.at[owner]
        return push(at, at, p_s.at[d], p_r.at[d], target, mp)

    for d in range(1, nz):
        start(query_push(d, z, z_dev(d)))
        start(column_push(d, z, z_dev(d)))

    def key_forward(shard, j, send, recv, queue, mp_index, which=x_slot):
        at = key_rows(which, k_start(shard, j), k_count)
        return push(at, at, send, recv, queue, mp_index)

    def next_rows(step):
        block = key_count // 3
        at = pl.ds(step * block, block)
        length = key_count * n_queue
        ids = me * key_count + step * block + lax.broadcasted_iota(jnp.int32, (block, 1), 0)
        offsets = ids - pointer_ref[0]
        offsets = jnp.where(offsets < 0, offsets + length, offsets)
        count = new_ref.shape[0]
        chosen = lax.broadcasted_iota(jnp.int32, (block, count), 1) == offsets
        taken = jnp.dot(
            jnp.where(chosen, 1.0, 0.0).astype(jnp.bfloat16), new_ref[...],
            preferred_element_type=jnp.float32,
        )
        held = keys[pl.ds(pl.multiple_of(slot * key_count + step * block, 16), block), :]
        next_ref[at, :] = jnp.where(offsets < count, taken, held.astype(jnp.float32)).astype(
            jnp.bfloat16
        )

    own_keys.wait()
    for step in range(3):
        next_rows(step)

    for j in range(KEY_CHUNKS):
        key_forward(mp, j, kx_s.at[j], kx_r.at[j], x_peer, mp).wait_recv()
        for d in range(1, n_mp):
            start(key_forward(mp, j, ky_s.at[d, j], ky_r.at[d, j], me, mp_dev(d)))
        start(key_forward(mp, j, kcx_s.at[j], kcx_r.at[j], core_peer, mp))
    for j in range(KEY_CHUNKS):
        for d in range(1, n_mp):
            shard = mp_dev(n_mp - d)
            key_forward(shard, j, ky_s.at[d, j], ky_r.at[d, j], me, mp).wait_recv()
            start(key_forward(shard, j, kcy_s.at[d, j], kcy_r.at[d, j], core_peer, mp))
    push(
        keys_ref, key_rows(core_slot, 0, key_count), kc_s.at[0], kc_r.at[0], core_peer, mp
    ).wait_recv()
    for j in range(KEY_CHUNKS):
        key_forward(mp, j, kcx_s.at[j], kcx_r.at[j], core_peer, mp, diag_slot).wait_recv()
        for d in range(1, n_mp):
            shard = mp_dev(n_mp - d)
            key_forward(
                shard, j, kcy_s.at[d, j], kcy_r.at[d, j], core_peer, mp, diag_slot
            ).wait_recv()

    for d in range(1, nz):
        source = lax.rem(z + nz - d, nz)
        query_push(d, source, me).wait_recv()
        column_push(d, source, me).wait_recv()

    factor = 2.0 / math.sqrt(width)
    total_rows = nz * rows
    total_keys = GROUP * key_count
    block = 256
    column = jnp.concatenate(
        [column_of(columns[i], 0, rows) for i in range(nz)], axis=0
    ) - z * total_keys

    def is_positive(step):
        ids = step * block + lax.broadcasted_iota(jnp.int32, (total_rows, block), 1)
        return ids == column

    def score_step(step, carry):
        peak, total, positive = carry
        at = pl.ds(pl.multiple_of(step * block, block), block)
        product = (
            lax.dot_general(
                queries[...], keys[at, :], (((1,), (1,)), ((), ())),
                preferred_element_type=jnp.float32,
            )
            * factor
        )
        scores[:, at] = product
        new_peak = jnp.maximum(peak, jnp.max(product, axis=1, keepdims=True))
        total = total * jnp.exp(peak - new_peak) + jnp.sum(
            jnp.exp(product - new_peak), axis=1, keepdims=True
        )
        positive = positive + jnp.sum(
            jnp.where(is_positive(step), product, 0.0), axis=1, keepdims=True
        )
        return new_peak, total, positive

    zero = jnp.zeros((total_rows, 1), jnp.float32)
    peak, total, positive = lax.fori_loop(
        0, total_keys // block, score_step, (zero - 1e30, zero, zero)
    )
    for i in range(nz):
        at = slice(i * rows, (i + 1) * rows)
        stats[z, i, 0:1, :] = row_of(peak[at])
        stats[z, i, 1:2, :] = row_of(total[at])
        stats[z, i, 2:3, :] = row_of(positive[at])

    def stats_push(d, owner, target):
        at = stats.at[owner]
        return push(at, at, st_s.at[d], st_r.at[d], target, mp)

    for d in range(1, nz):
        start(stats_push(d, z, z_dev(d)))
    for d in range(1, nz):
        stats_push(d, lax.rem(z + nz - d, nz), me).wait_recv()

    top = stats[0, :, 0, :]
    for i in range(1, nz):
        top = jnp.maximum(top, stats[i, :, 0, :])
    whole = jnp.zeros_like(top)
    found = jnp.zeros_like(top)
    for i in range(nz):
        whole = whole + stats[i, :, 1, :] * jnp.exp(stats[i, :, 0, :] - top)
        found = found + stats[i, :, 2, :]
    log_rows = top + jnp.log(jnp.maximum(whole, 1e-30))
    losses = log_rows - found
    loss_line = jnp.zeros((1, LANES), jnp.float32)
    for i in range(nz):
        loss_line = loss_line + jnp.where(z == i, losses[i : i + 1, :], 0.0)
    loss_ref[...] = jnp.broadcast_to(loss_line, loss_ref.shape)
    log_total = jnp.concatenate(
        [column_of(log_rows[i : i + 1, :], 0, rows) for i in range(nz)], axis=0
    )

    @pl.loop(0, total_keys // block)
    def _(step):
        at = pl.ds(pl.multiple_of(step * block, block), block)
        probs[:, at] = (
            jnp.exp(scores[:, at] - log_total) - jnp.where(is_positive(step), 1.0, 0.0)
        ).astype(jnp.bfloat16)

    n_blocks = width // block

    def grad_push(d, c, source, owner, target):
        return push(
            partial.at[c, z_rows(owner), :], arrived.at[source, c],
            g_s.at[d, c], g_r.at[d, c], target, mp,
        )

    for c in range(n_blocks):
        partial[c] = jnp.dot(
            probs[...], keys[:, c * block : (c + 1) * block], preferred_element_type=jnp.float32
        ).astype(jnp.bfloat16)
        for d in range(1, nz):
            owner = lax.rem(z + d, nz)
            start(grad_push(d, c, z, owner, z_dev(d)))

    scaled = []
    inner = jnp.zeros((rows, 1), jnp.float32)
    for c in range(n_blocks):
        summed = partial[c, own_rows, :].astype(jnp.float32)
        for d in range(1, nz):
            source = lax.rem(z + nz - d, nz)
            grad_push(d, c, source, z, me).wait_recv()
            summed = summed + arrived[source, c].astype(jnp.float32)
        at = slice(c * block, (c + 1) * block)
        block_scaled = gain_ref[:, at] * (summed * (16.0 * factor))
        scaled.append(block_scaled)
        inner = inner + jnp.sum(block_scaled * hidden[:, at], axis=1, keepdims=True)
    inner = inverse_rms * inverse_rms * inverse_rms * inner / width
    hidden_grad = jnp.concatenate(
        [
            (inverse_rms * scaled[c] - hidden[:, c * block : (c + 1) * block] * inner).astype(
                jnp.bfloat16
            )
            for c in range(n_blocks)
        ],
        axis=1,
    )
    result = jnp.zeros((rows, width), jnp.float32)
    for m in range(n_mp):
        result = result + lax.dot_general(
            hidden_grad[:, m * part_width : (m + 1) * part_width], weights_in[m],
            (((1,), (1,)), ((), ())), preferred_element_type=jnp.float32,
        )
    grad_ref[...] = result.astype(jnp.bfloat16)
    for copy in sends:
        copy.wait_send()


def shards(n_queue, n_mp, speech, weight, norm_gain, queue_keys, new_keys, pointer, positives):
    rows, width = speech.shape
    key_count = queue_keys.shape[0]
    nz = n_queue // GROUP
    vmem = pl.BlockSpec(memory_space=pltpu.VMEM)
    anywhere = pl.BlockSpec(memory_space=pl.ANY)
    dma = pltpu.SemaphoreType.DMA
    bf16, f32 = jnp.bfloat16, jnp.float32
    line = jnp.broadcast_to(jnp.pad(positives, (0, LANES - rows))[None, :], (8, LANES))
    scratch = [
        pltpu.VMEM((GROUP * key_count, width), bf16),
        pltpu.VMEM((n_mp, width, width // n_mp), bf16),
        pltpu.VMEM((nz * rows, width), bf16),
        pltpu.VMEM((nz, 8, LANES), jnp.int32),
        pltpu.VMEM((nz * rows, GROUP * key_count), f32),
        pltpu.VMEM((nz * rows, GROUP * key_count), bf16),
        pltpu.VMEM((rows, width), f32),
        pltpu.VMEM((width // 256, nz * rows, 256), bf16),
        pltpu.VMEM((nz, width // 256, rows, 256), bf16),
        pltpu.VMEM((nz, nz, 8, LANES), f32),
        dma((2,)),
    ]
    scratch += [dma((n_mp, WEIGHT_CHUNKS))] * 10
    scratch += [dma((1,))] * 2 + [dma((KEY_CHUNKS,))] * 2 + [dma((n_mp, KEY_CHUNKS))] * 2
    scratch += [dma((KEY_CHUNKS,))] * 2 + [dma((n_mp, KEY_CHUNKS))] * 2
    scratch += [dma((nz,))] * 6 + [dma((nz, width // 256))] * 2
    loss, grad, queue_next = pl.pallas_call(
        functools.partial(step_kernel, n_queue, n_mp),
        out_shape=(
            jax.ShapeDtypeStruct((8, LANES), f32),
            jax.ShapeDtypeStruct((rows, width), bf16),
            jax.ShapeDtypeStruct((key_count, width), bf16),
        ),
        in_specs=[vmem, anywhere, vmem, anywhere, vmem, pl.BlockSpec(memory_space=pltpu.SMEM), vmem],
        out_specs=(vmem, vmem, vmem),
        scratch_shapes=scratch,
        compiler_params=pltpu.CompilerParams(
            collective_id=0, has_side_effects=True, vmem_limit_bytes=52 * 1024 * 1024
        ),
        name="contrast_step",
    )(speech, weight, norm_gain[None, :], queue_keys, new_keys, pointer, line)
    return loss[0, :rows], grad, queue_next


def solution(mesh):
    n_queue, n_mp = mesh.shape["queue"], mesh.shape["mp"]
    return jax.shard_map(
        functools.partial(shards, n_queue, n_mp),
        mesh=mesh,
        in_specs=(
            P(("queue", "mp"), None),
            P(None, "mp"),
            P(),
            P("queue", None),
            P(),
            P(),
            P(("queue", "mp")),
        ),
        out_specs=(P(("queue", "mp")), P(("queue", "mp"), None), P("queue", None)),
        check_vma=False,
    )
```

```python
import functools
import math

import jax
import jax.numpy as jnp
from jax import lax
from jax.experimental import pallas as pl
from jax.experimental.pallas import tpu as pltpu
from jax.sharding import PartitionSpec as P

MESH = pl.DeviceIdType.MESH
GROUP = 4
WEIGHT_CHUNKS = 4
KEY_CHUNKS = 6
LANES = 128


def column_of(tile, row, count):
    line = jnp.broadcast_to(tile[row : row + 1, :], (LANES, LANES))
    eye = lax.broadcasted_iota(jnp.int32, (LANES, LANES), 0) == lax.broadcasted_iota(
        jnp.int32, (LANES, LANES), 1
    )
    return jnp.sum(jnp.where(eye, line, jnp.zeros_like(line)), axis=1, keepdims=True)[:count]


def row_of(column):
    count = column.shape[0]
    wide = jnp.broadcast_to(column, (count, LANES))
    eye = lax.broadcasted_iota(jnp.int32, (count, LANES), 0) == lax.broadcasted_iota(
        jnp.int32, (count, LANES), 1
    )
    return jnp.sum(jnp.where(eye, wide, jnp.zeros_like(wide)), axis=0, keepdims=True)


def step_kernel(
    n_queue,
    n_mp,
    speech_hbm,
    weight_ref,
    gain_ref,
    keys_ref,
    new_hbm,
    pointer_ref,
    positives_ref,
    loss_ref,
    grad_ref,
    taken_ref,
    speech_ref,
    new_ref,
    keys,
    weights_in,
    queries,
    columns,
    scores,
    probs,
    hidden,
    partial,
    arrived,
    stats,
    wide_peak,
    wide_total,
    wide_positive,
    wide_column,
    local_sem,
    wy_s, wy_r, wx_s, wx_r, wcy_s, wcy_r, wcx_s, wcx_r, wco_s, wco_r,
    kc_s, kc_r, kx_s, kx_r, ky_s, ky_r, kcx_s, kcx_r, kcy_s, kcy_r,
    q_s, q_r, p_s, p_r, st_s, st_r, g_s, g_r,
):
    rows, width = speech_ref.shape
    key_count = keys_ref.shape[0]
    nz = n_queue // GROUP
    me = lax.axis_index("queue")
    mp = lax.axis_index("mp")
    z = me // GROUP
    slot = me % GROUP
    x = slot // 2
    core = slot % 2
    core_peer = me + 1 - 2 * core
    x_peer = me + 2 - 4 * x
    core_slot = slot + 1 - 2 * core
    x_slot = slot + 2 - 4 * x
    diag_slot = core_slot + 2 - 4 * x

    def z_dev(distance):
        return lax.rem(z + distance, nz) * GROUP + slot

    def mp_dev(distance):
        return lax.rem(mp + distance, n_mp)

    def push(src, dst, send, recv, queue, mp_index):
        return pltpu.make_async_remote_copy(
            src_ref=src, dst_ref=dst, send_sem=send, recv_sem=recv,
            device_id=(queue, mp_index), device_id_type=MESH,
        )

    barrier = pltpu.get_barrier_semaphore()
    peers = [(core_peer, mp), (x_peer, mp)]
    peers += [(me, mp_dev(d)) for d in range(1, n_mp)]
    peers += [(z_dev(d), mp) for d in range(1, nz)]
    for peer in peers:
        pl.semaphore_signal(barrier, inc=1, device_id=peer, device_id_type=MESH)

    def key_rows(which, start, count):
        return keys.at[pl.ds(pl.multiple_of(which * key_count + start, 16), count), :]

    own_keys = pltpu.make_async_copy(keys_ref, key_rows(slot, 0, key_count), local_sem.at[0])
    own_weight = pltpu.make_async_copy(weight_ref, weights_in.at[mp], local_sem.at[1])
    own_speech = pltpu.make_async_copy(speech_hbm, speech_ref, local_sem.at[2])
    own_new = pltpu.make_async_copy(new_hbm, new_ref, local_sem.at[3])
    own_weight.start()
    own_speech.start()
    own_keys.start()
    own_new.start()
    pl.semaphore_wait(barrier, len(peers))

    sends = []

    def start(copy):
        copy.start()
        sends.append(copy)

    w_count = width // GROUP // WEIGHT_CHUNKS

    def w_push(dist, quarter, j, shard, sems, queue, mp_index, src=None):
        at = pl.ds(pl.multiple_of(quarter * (width // GROUP) + j * w_count, 16), w_count)
        dst = weights_in.at[shard, at, :]
        return push(
            dst if src is None else src.at[at, :], dst,
            sems[0].at[dist, j], sems[1].at[dist, j], queue, mp_index,
        )

    for j in range(WEIGHT_CHUNKS):
        for d in range(1, n_mp):
            start(w_push(d, slot, j, mp, (wy_s, wy_r), me, mp_dev(d), weight_ref))

    part = key_count // n_mp
    k_count = part // KEY_CHUNKS

    def k_start(shard, j):
        return shard * part + j * k_count

    def key_x(j):
        at = k_start(mp, j)
        return push(
            keys_ref.at[pl.ds(pl.multiple_of(at, 16), k_count), :], key_rows(slot, at, k_count),
            kx_s.at[j], kx_r.at[j], x_peer, mp,
        )

    def key_forward(shard, j, send, recv, queue, mp_index, which=x_slot):
        at = key_rows(which, k_start(shard, j), k_count)
        return push(at, at, send, recv, queue, mp_index)

    def key_arrive_x(j):
        key_forward(mp, j, kx_s.at[j], kx_r.at[j], x_peer, mp).wait_recv()
        for d in range(1, n_mp):
            start(key_forward(mp, j, ky_s.at[d, j], ky_r.at[d, j], me, mp_dev(d)))
        start(key_forward(mp, j, kcx_s.at[j], kcx_r.at[j], core_peer, mp))

    def key_arrive_y(j):
        for d in range(1, n_mp):
            shard = mp_dev(n_mp - d)
            key_forward(shard, j, ky_s.at[d, j], ky_r.at[d, j], me, mp).wait_recv()
            start(key_forward(shard, j, kcy_s.at[d, j], kcy_r.at[d, j], core_peer, mp))

    start(key_x(0))
    start(push(keys_ref, key_rows(slot, 0, key_count), kc_s.at[0], kc_r.at[0], core_peer, mp))

    for j in range(WEIGHT_CHUNKS):
        for d in range(1, n_mp):
            shard = mp_dev(n_mp - d)
            w_push(d, slot, j, shard, (wy_s, wy_r), me, mp).wait_recv()
            start(w_push(d, slot, j, shard, (wx_s, wx_r), x_peer, mp))
            start(w_push(d, slot, j, shard, (wcy_s, wcy_r), core_peer, mp))
    for j in range(1, KEY_CHUNKS):
        start(key_x(j))
    for j in range(WEIGHT_CHUNKS):
        for d in range(1, n_mp):
            shard = mp_dev(n_mp - d)
            w_push(d, x_slot, j, shard, (wx_s, wx_r), x_peer, mp).wait_recv()
            start(w_push(d, x_slot, j, shard, (wcx_s, wcx_r), core_peer, mp))
    key_arrive_x(0)
    own_speech.wait()
    own_weight.wait()
    for j in range(WEIGHT_CHUNKS):
        for d in range(1, n_mp):
            shard = mp_dev(n_mp - d)
            w_push(d, core_slot, j, shard, (wcy_s, wcy_r), core_peer, mp).wait_recv()
            w_push(d, diag_slot, j, shard, (wcx_s, wcx_r), core_peer, mp).wait_recv()

    part_width = width // n_mp
    for m in range(n_mp):
        hidden[:, m * part_width : (m + 1) * part_width] = jnp.dot(
            speech_ref[...], weights_in[m], preferred_element_type=jnp.float32
        )
    encoded = hidden[...]
    inverse_rms = lax.rsqrt(jnp.mean(encoded * encoded, axis=1, keepdims=True) + 1e-06)
    own_rows = pl.ds(pl.multiple_of(z * rows, 16), rows)
    queries[own_rows, :] = (encoded * inverse_rms * gain_ref[...]).astype(jnp.bfloat16)
    columns[z, 0:1, 0:rows] = positives_ref[...]

    def z_rows(index):
        return pl.ds(pl.multiple_of(index * rows, 16), rows)

    def query_push(d, owner, target):
        at = queries.at[z_rows(owner), :]
        return push(at, at, q_s.at[d], q_r.at[d], target, mp)

    def column_push(d, owner, target):
        at = columns.at[owner]
        return push(at, at, p_s.at[d], p_r.at[d], target, mp)

    for d in range(1, nz):
        start(query_push(d, z, z_dev(d)))
        start(column_push(d, z, z_dev(d)))

    def take_rows(step):
        block = key_count // 3
        at = pl.ds(step * block, block)
        length = key_count * n_queue
        ids = me * key_count + step * block + lax.broadcasted_iota(jnp.int32, (block, 1), 0)
        offsets = ids - pointer_ref[0]
        offsets = jnp.where(offsets < 0, offsets + length, offsets)
        count = new_ref.shape[0]
        chosen = lax.broadcasted_iota(jnp.int32, (block, count), 1) == offsets
        taken = jnp.dot(
            jnp.where(chosen, 1.0, 0.0).astype(jnp.bfloat16), new_ref[...],
            preferred_element_type=jnp.float32,
        )
        taken_ref[at, :] = taken.astype(jnp.bfloat16)

    own_keys.wait()
    for j in range(1, KEY_CHUNKS):
        key_arrive_x(j)
        if j == 3:
            own_new.wait()
            for step in range(3):
                take_rows(step)
    for j in range(KEY_CHUNKS):
        key_arrive_y(j)
    push(
        keys_ref, key_rows(core_slot, 0, key_count), kc_s.at[0], kc_r.at[0], core_peer, mp
    ).wait_recv()
    for j in range(KEY_CHUNKS):
        key_forward(mp, j, kcx_s.at[j], kcx_r.at[j], core_peer, mp, diag_slot).wait_recv()
        for d in range(1, n_mp):
            shard = mp_dev(n_mp - d)
            key_forward(
                shard, j, kcy_s.at[d, j], kcy_r.at[d, j], core_peer, mp, diag_slot
            ).wait_recv()

    for d in range(1, nz):
        source = lax.rem(z + nz - d, nz)
        query_push(d, source, me).wait_recv()
        column_push(d, source, me).wait_recv()

    factor = 2.0 / math.sqrt(width)
    total_rows = nz * rows
    total_keys = GROUP * key_count
    block = 256
    for i in range(nz):
        wide_column[i * rows : (i + 1) * rows, :] = jnp.broadcast_to(
            column_of(columns[i], 0, rows) - z * total_keys, (rows, LANES)
        )
    wide_peak[...] = jnp.full((total_rows, LANES), -1e30, jnp.float32)
    wide_total[...] = jnp.zeros((total_rows, LANES), jnp.float32)
    wide_positive[...] = jnp.zeros((total_rows, LANES), jnp.float32)

    def is_positive(start):
        ids = start + lax.broadcasted_iota(jnp.int32, (total_rows, LANES), 1)
        return ids == wide_column[...]

    @pl.loop(0, total_keys // block)
    def _(step):
        at = pl.ds(pl.multiple_of(step * block, block), block)
        product = (
            lax.dot_general(
                queries[...], keys[at, :], (((1,), (1,)), ((), ())),
                preferred_element_type=jnp.float32,
            )
            * factor
        )
        scores[:, at] = product
        peak = wide_peak[...]
        positive = wide_positive[...]
        for half in range(block // LANES):
            piece = product[:, half * LANES : (half + 1) * LANES]
            peak = jnp.maximum(peak, piece)
            positive = positive + jnp.where(is_positive(step * block + half * LANES), piece, 0.0)
        wide_peak[...] = peak
        wide_positive[...] = positive

    peak = jnp.max(wide_peak[...], axis=1, keepdims=True)
    wide_peak[...] = jnp.broadcast_to(peak, (total_rows, LANES))

    @pl.loop(0, total_keys // block)
    def _(step):
        total = wide_total[...]
        for half in range(block // LANES):
            at = pl.ds(pl.multiple_of(step * block + half * LANES, LANES), LANES)
            power = jnp.exp(scores[:, at] - wide_peak[...])
            scores[:, at] = power
            total = total + power
        wide_total[...] = total

    total = jnp.sum(wide_total[...], axis=1, keepdims=True)
    positive = jnp.sum(wide_positive[...], axis=1, keepdims=True)
    for i in range(nz):
        at = slice(i * rows, (i + 1) * rows)
        stats[z, i, 0:1, :] = row_of(peak[at])
        stats[z, i, 1:2, :] = row_of(total[at])
        stats[z, i, 2:3, :] = row_of(positive[at])

    def stats_push(d, owner, target):
        at = stats.at[owner]
        return push(at, at, st_s.at[d], st_r.at[d], target, mp)

    for d in range(1, nz):
        start(stats_push(d, z, z_dev(d)))
    for d in range(1, nz):
        stats_push(d, lax.rem(z + nz - d, nz), me).wait_recv()

    top = stats[0, :, 0, :]
    for i in range(1, nz):
        top = jnp.maximum(top, stats[i, :, 0, :])
    whole = jnp.zeros_like(top)
    found = jnp.zeros_like(top)
    for i in range(nz):
        whole = whole + stats[i, :, 1, :] * jnp.exp(stats[i, :, 0, :] - top)
        found = found + stats[i, :, 2, :]
    log_rows = top + jnp.log(jnp.maximum(whole, 1e-30))
    losses = log_rows - found
    loss_line = jnp.zeros((1, LANES), jnp.float32)
    for i in range(nz):
        loss_line = loss_line + jnp.where(z == i, losses[i : i + 1, :], 0.0)
    loss_ref[...] = jnp.broadcast_to(loss_line, loss_ref.shape)
    log_total = jnp.concatenate(
        [column_of(log_rows[i : i + 1, :], 0, rows) for i in range(nz)], axis=0
    )

    wide_total[...] = jnp.broadcast_to(jnp.exp(peak - log_total), (total_rows, LANES))

    @pl.loop(0, total_keys // block)
    def _(step):
        for half in range(block // LANES):
            start_at = pl.multiple_of(step * block + half * LANES, LANES)
            at = pl.ds(start_at, LANES)
            probs[:, at] = (
                scores[:, at] * wide_total[...] - jnp.where(is_positive(start_at), 1.0, 0.0)
            ).astype(jnp.bfloat16)

    n_blocks = width // block

    def grad_push(d, c, source, owner, target):
        return push(
            partial.at[c, z_rows(owner), :], arrived.at[source, c],
            g_s.at[d, c], g_r.at[d, c], target, mp,
        )

    for c in range(n_blocks):
        partial[c] = jnp.dot(
            probs[...], keys[:, c * block : (c + 1) * block], preferred_element_type=jnp.float32
        ).astype(jnp.bfloat16)
        for d in range(1, nz):
            owner = lax.rem(z + d, nz)
            start(grad_push(d, c, z, owner, z_dev(d)))

    scaled = []
    inner = jnp.zeros((rows, 1), jnp.float32)
    for c in range(n_blocks):
        summed = partial[c, own_rows, :].astype(jnp.float32)
        for d in range(1, nz):
            source = lax.rem(z + nz - d, nz)
            grad_push(d, c, source, z, me).wait_recv()
            summed = summed + arrived[source, c].astype(jnp.float32)
        at = slice(c * block, (c + 1) * block)
        block_scaled = gain_ref[:, at] * (summed * (16.0 * factor))
        scaled.append(block_scaled)
        inner = inner + jnp.sum(block_scaled * hidden[:, at], axis=1, keepdims=True)
    inner = inverse_rms * inverse_rms * inverse_rms * inner / width
    hidden_grad = jnp.concatenate(
        [
            (inverse_rms * scaled[c] - hidden[:, c * block : (c + 1) * block] * inner).astype(
                jnp.bfloat16
            )
            for c in range(n_blocks)
        ],
        axis=1,
    )
    result = jnp.zeros((rows, width), jnp.float32)
    for m in range(n_mp):
        result = result + lax.dot_general(
            hidden_grad[:, m * part_width : (m + 1) * part_width], weights_in[m],
            (((1,), (1,)), ((), ())), preferred_element_type=jnp.float32,
        )
    grad_ref[...] = result.astype(jnp.bfloat16)
    for copy in sends:
        copy.wait_send()


def shards(n_queue, n_mp, speech, weight, norm_gain, queue_keys, new_keys, pointer, positives):
    rows, width = speech.shape
    key_count = queue_keys.shape[0]
    nz = n_queue // GROUP
    vmem = pl.BlockSpec(memory_space=pltpu.VMEM)
    anywhere = pl.BlockSpec(memory_space=pl.ANY)
    dma = pltpu.SemaphoreType.DMA
    bf16, f32 = jnp.bfloat16, jnp.float32
    scratch = [
        pltpu.VMEM((rows, width), bf16),
        pltpu.VMEM(new_keys.shape, bf16),
        pltpu.VMEM((GROUP * key_count, width), bf16),
        pltpu.VMEM((n_mp, width, width // n_mp), bf16),
        pltpu.VMEM((nz * rows, width), bf16),
        pltpu.VMEM((nz, 8, LANES), jnp.int32),
        pltpu.VMEM((nz * rows, GROUP * key_count), f32),
        pltpu.VMEM((nz * rows, GROUP * key_count), bf16),
        pltpu.VMEM((rows, width), f32),
        pltpu.VMEM((width // 256, nz * rows, 256), bf16),
        pltpu.VMEM((nz, width // 256, rows, 256), bf16),
        pltpu.VMEM((nz, nz, 8, LANES), f32),
        pltpu.VMEM((nz * rows, LANES), f32),
        pltpu.VMEM((nz * rows, LANES), f32),
        pltpu.VMEM((nz * rows, LANES), f32),
        pltpu.VMEM((nz * rows, LANES), jnp.int32),
        dma((4,)),
    ]
    scratch += [dma((n_mp, WEIGHT_CHUNKS))] * 10
    scratch += [dma((1,))] * 2 + [dma((KEY_CHUNKS,))] * 2 + [dma((n_mp, KEY_CHUNKS))] * 2
    scratch += [dma((KEY_CHUNKS,))] * 2 + [dma((n_mp, KEY_CHUNKS))] * 2
    scratch += [dma((nz,))] * 6 + [dma((nz, width // 256))] * 2
    loss, grad, taken = pl.pallas_call(
        functools.partial(step_kernel, n_queue, n_mp),
        out_shape=(
            jax.ShapeDtypeStruct((8, LANES), f32),
            jax.ShapeDtypeStruct((rows, width), bf16),
            jax.ShapeDtypeStruct((key_count, width), bf16),
        ),
        in_specs=[anywhere, anywhere, vmem, anywhere, anywhere, pl.BlockSpec(memory_space=pltpu.SMEM), vmem],
        out_specs=(vmem, vmem, vmem),
        scratch_shapes=scratch,
        compiler_params=pltpu.CompilerParams(
            collective_id=0, has_side_effects=True, vmem_limit_bytes=63 * 1024 * 1024
        ),
        name="contrast_step",
    )(speech, weight, norm_gain[None, :], queue_keys, new_keys, pointer, positives[None, :])
    length = key_count * n_queue
    ids = lax.axis_index("queue") * key_count + lax.broadcasted_iota(jnp.int32, (key_count, 1), 0)
    offsets = ids - pointer[0]
    offsets = jnp.where(offsets < 0, offsets + length, offsets)
    queue_next = jnp.where(offsets < new_keys.shape[0], taken, queue_keys)
    return loss[0, :rows], grad, queue_next


def solution(mesh):
    n_queue, n_mp = mesh.shape["queue"], mesh.shape["mp"]
    return jax.shard_map(
        functools.partial(shards, n_queue, n_mp),
        mesh=mesh,
        in_specs=(
            P(("queue", "mp"), None),
            P(None, "mp"),
            P(),
            P("queue", None),
            P(),
            P(),
            P(("queue", "mp")),
        ),
        out_specs=(P(("queue", "mp")), P(("queue", "mp"), None), P("queue", None)),
        check_vma=False,
    )
```

```python
import functools
import math

import jax
import jax.numpy as jnp
from jax import lax
from jax.experimental import pallas as pl
from jax.experimental.pallas import tpu as pltpu
from jax.sharding import PartitionSpec as P

MESH = pl.DeviceIdType.MESH
GROUP = 4
WEIGHT_CHUNKS = 4
KEY_CHUNKS = 6
LANES = 128


def column_of(tile, row, count):
    line = jnp.broadcast_to(tile[row : row + 1, :], (LANES, LANES))
    eye = lax.broadcasted_iota(jnp.int32, (LANES, LANES), 0) == lax.broadcasted_iota(
        jnp.int32, (LANES, LANES), 1
    )
    return jnp.sum(jnp.where(eye, line, jnp.zeros_like(line)), axis=1, keepdims=True)[:count]


def row_of(column):
    count = column.shape[0]
    wide = jnp.broadcast_to(column, (count, LANES))
    eye = lax.broadcasted_iota(jnp.int32, (count, LANES), 0) == lax.broadcasted_iota(
        jnp.int32, (count, LANES), 1
    )
    return jnp.sum(jnp.where(eye, wide, jnp.zeros_like(wide)), axis=0, keepdims=True)


def step_kernel(
    n_queue,
    n_mp,
    speech_hbm,
    weight_ref,
    gain_ref,
    keys_ref,
    new_hbm,
    pointer_ref,
    positives_ref,
    loss_ref,
    grad_ref,
    next_ref,
    speech_ref,
    new_ref,
    next_rows,
    keys,
    weights_in,
    queries,
    columns,
    scores,
    probs,
    hidden,
    partial,
    arrived,
    stats,
    wide_peak,
    wide_total,
    wide_positive,
    wide_column,
    local_sem,
    wy_s, wy_r, wx_s, wx_r, wcy_s, wcy_r, wcx_s, wcx_r, wco_s, wco_r,
    kc_s, kc_r, kx_s, kx_r, ky_s, ky_r, kcx_s, kcx_r, kcy_s, kcy_r,
    q_s, q_r, p_s, p_r, st_s, st_r, g_s, g_r,
):
    rows, width = speech_ref.shape
    key_count = keys_ref.shape[0]
    nz = n_queue // GROUP
    me = lax.axis_index("queue")
    mp = lax.axis_index("mp")
    z = me // GROUP
    slot = me % GROUP
    x = slot // 2
    core = slot % 2
    core_peer = me + 1 - 2 * core
    x_peer = me + 2 - 4 * x
    core_slot = slot + 1 - 2 * core
    x_slot = slot + 2 - 4 * x
    diag_slot = core_slot + 2 - 4 * x

    def z_dev(distance):
        return lax.rem(z + distance, nz) * GROUP + slot

    def mp_dev(distance):
        return lax.rem(mp + distance, n_mp)

    def push(src, dst, send, recv, queue, mp_index):
        return pltpu.make_async_remote_copy(
            src_ref=src, dst_ref=dst, send_sem=send, recv_sem=recv,
            device_id=(queue, mp_index), device_id_type=MESH,
        )

    barrier = pltpu.get_barrier_semaphore()
    peers = [(core_peer, mp), (x_peer, mp)]
    peers += [(me, mp_dev(d)) for d in range(1, n_mp)]
    peers += [(z_dev(d), mp) for d in range(1, nz)]
    for peer in peers:
        pl.semaphore_signal(barrier, inc=1, device_id=peer, device_id_type=MESH)

    def key_rows(which, start, count):
        return keys.at[pl.ds(pl.multiple_of(which * key_count + start, 16), count), :]

    own_keys = pltpu.make_async_copy(keys_ref, key_rows(slot, 0, key_count), local_sem.at[0])
    own_weight = pltpu.make_async_copy(weight_ref, weights_in.at[mp], local_sem.at[1])
    own_speech = pltpu.make_async_copy(speech_hbm, speech_ref, local_sem.at[2])
    own_new = pltpu.make_async_copy(new_hbm, new_ref, local_sem.at[3])
    own_weight.start()
    own_speech.start()
    own_keys.start()
    own_new.start()
    pl.semaphore_wait(barrier, len(peers))

    sends = []
    guarded = []

    def start(copy):
        copy.start()
        sends.append(copy)

    w_count = width // GROUP // WEIGHT_CHUNKS

    def w_push(dist, quarter, j, shard, sems, queue, mp_index, src=None):
        at = pl.ds(pl.multiple_of(quarter * (width // GROUP) + j * w_count, 16), w_count)
        dst = weights_in.at[shard, at, :]
        return push(
            dst if src is None else src.at[at, :], dst,
            sems[0].at[dist, j], sems[1].at[dist, j], queue, mp_index,
        )

    for j in range(WEIGHT_CHUNKS):
        for d in range(1, n_mp):
            start(w_push(d, slot, j, mp, (wy_s, wy_r), me, mp_dev(d), weight_ref))

    part = key_count // n_mp
    k_count = part // KEY_CHUNKS

    def k_start(shard, j):
        return shard * part + j * k_count

    def key_x(j):
        at = k_start(mp, j)
        return push(
            keys_ref.at[pl.ds(pl.multiple_of(at, 16), k_count), :], key_rows(slot, at, k_count),
            kx_s.at[j], kx_r.at[j], x_peer, mp,
        )

    def key_forward(shard, j, send, recv, queue, mp_index, which=x_slot):
        at = key_rows(which, k_start(shard, j), k_count)
        return push(at, at, send, recv, queue, mp_index)

    def key_arrive_x(j):
        key_forward(mp, j, kx_s.at[j], kx_r.at[j], x_peer, mp).wait_recv()
        for d in range(1, n_mp):
            start(key_forward(mp, j, ky_s.at[d, j], ky_r.at[d, j], me, mp_dev(d)))
        start(key_forward(mp, j, kcx_s.at[j], kcx_r.at[j], core_peer, mp))

    def key_arrive_y(j):
        for d in range(1, n_mp):
            shard = mp_dev(n_mp - d)
            key_forward(shard, j, ky_s.at[d, j], ky_r.at[d, j], me, mp).wait_recv()
            start(key_forward(shard, j, kcy_s.at[d, j], kcy_r.at[d, j], core_peer, mp))

    start(key_x(0))
    start(push(keys_ref, key_rows(slot, 0, key_count), kc_s.at[0], kc_r.at[0], core_peer, mp))

    for j in range(WEIGHT_CHUNKS):
        for d in range(1, n_mp):
            shard = mp_dev(n_mp - d)
            w_push(d, slot, j, shard, (wy_s, wy_r), me, mp).wait_recv()
            start(w_push(d, slot, j, shard, (wx_s, wx_r), x_peer, mp))
            start(w_push(d, slot, j, shard, (wcy_s, wcy_r), core_peer, mp))
    for j in range(1, KEY_CHUNKS):
        start(key_x(j))
    for j in range(WEIGHT_CHUNKS):
        for d in range(1, n_mp):
            shard = mp_dev(n_mp - d)
            w_push(d, x_slot, j, shard, (wx_s, wx_r), x_peer, mp).wait_recv()
            start(w_push(d, x_slot, j, shard, (wcx_s, wcx_r), core_peer, mp))
    key_arrive_x(0)
    own_speech.wait()
    own_weight.wait()
    for j in range(WEIGHT_CHUNKS):
        for d in range(1, n_mp):
            shard = mp_dev(n_mp - d)
            w_push(d, core_slot, j, shard, (wcy_s, wcy_r), core_peer, mp).wait_recv()
            w_push(d, diag_slot, j, shard, (wcx_s, wcx_r), core_peer, mp).wait_recv()

    part_width = width // n_mp
    for m in range(n_mp):
        hidden[:, m * part_width : (m + 1) * part_width] = jnp.dot(
            speech_ref[...], weights_in[m], preferred_element_type=jnp.float32
        )
    encoded = hidden[...]
    inverse_rms = lax.rsqrt(jnp.mean(encoded * encoded, axis=1, keepdims=True) + 1e-06)
    own_rows = pl.ds(pl.multiple_of(z * rows, 16), rows)
    queries[own_rows, :] = (encoded * inverse_rms * gain_ref[...]).astype(jnp.bfloat16)
    columns[z, 0:1, 0:rows] = positives_ref[...]

    def z_rows(index):
        return pl.ds(pl.multiple_of(index * rows, 16), rows)

    has_left, has_right = z > 0, z < nz - 1
    halves = 2

    def guarded_start(condition, make):
        @pl.when(condition)
        def _():
            make().start()

        guarded.append((condition, make))

    def query_push(way, distance, half, owner, target):
        at = queries.at[
            pl.ds(pl.multiple_of(owner * rows + half * (rows // halves), 16), rows // halves), :
        ]
        return push(
            at, at, q_s.at[way, distance, half], q_r.at[way, distance, half],
            target * GROUP + slot, mp,
        )

    def column_push(d, owner, target):
        at = columns.at[owner]
        return push(at, at, p_s.at[d], p_r.at[d], target, mp)

    for half in range(halves):
        guarded_start(has_right, functools.partial(query_push, 0, 1, half, z, z + 1))
        guarded_start(has_left, functools.partial(query_push, 1, 1, half, z, z - 1))
    for d in range(1, nz):
        start(column_push(d, z, z_dev(d)))

    def query_arrive(distance, half):
        for way, there, onward, step in ((0, z >= distance, has_right, 1), (1, z + distance < nz, has_left, -1)):
            owner = z - step * distance

            @pl.when(there)
            def _():
                query_push(way, distance, half, owner, z).wait_recv()

            if distance + 1 < nz:
                guarded_start(
                    there & onward,
                    functools.partial(query_push, way, distance + 1, half, owner, z + step),
                )

    def take_rows(step):
        block = key_count // 3
        at = pl.ds(step * block, block)
        length = key_count * n_queue
        ids = me * key_count + step * block + lax.broadcasted_iota(jnp.int32, (block, 1), 0)
        offsets = ids - pointer_ref[0]
        offsets = jnp.where(offsets < 0, offsets + length, offsets)
        count = new_ref.shape[0]
        chosen = lax.broadcasted_iota(jnp.int32, (block, count), 1) == offsets
        taken = jnp.dot(
            jnp.where(chosen, 1.0, 0.0).astype(jnp.bfloat16), new_ref[...],
            preferred_element_type=jnp.float32,
        )
        held = keys[pl.ds(pl.multiple_of(slot * key_count + step * block, 16), block), :]
        next_rows[at, :] = jnp.where(offsets < count, taken, held.astype(jnp.float32)).astype(
            jnp.bfloat16
        )

    own_keys.wait()
    hops = [(distance, half) for distance in range(1, nz) for half in range(halves)]
    for j in range(1, KEY_CHUNKS):
        key_arrive_x(j)
        if j == 1:
            own_new.wait()
            for step in range(3):
                take_rows(step)
            next_out = pltpu.make_async_copy(next_rows, next_ref, local_sem.at[4])
            next_out.start()
        if j > 2:
            query_arrive(*hops.pop(0))
            key_arrive_y(j - 3)
    for j in range(KEY_CHUNKS - 3, KEY_CHUNKS):
        query_arrive(*hops.pop(0)) if hops else None
        key_arrive_y(j)
    for hop in hops:
        query_arrive(*hop)
    push(
        keys_ref, key_rows(core_slot, 0, key_count), kc_s.at[0], kc_r.at[0], core_peer, mp
    ).wait_recv()
    for j in range(KEY_CHUNKS):
        key_forward(mp, j, kcx_s.at[j], kcx_r.at[j], core_peer, mp, diag_slot).wait_recv()
        for d in range(1, n_mp):
            shard = mp_dev(n_mp - d)
            key_forward(
                shard, j, kcy_s.at[d, j], kcy_r.at[d, j], core_peer, mp, diag_slot
            ).wait_recv()

    for d in range(1, nz):
        source = lax.rem(z + nz - d, nz)
        column_push(d, source, me).wait_recv()

    factor = 2.0 / math.sqrt(width)
    total_rows = nz * rows
    total_keys = GROUP * key_count
    block = 256
    for i in range(nz):
        wide_column[i * rows : (i + 1) * rows, :] = jnp.broadcast_to(
            column_of(columns[i], 0, rows) - z * total_keys, (rows, LANES)
        )
    wide_peak[...] = jnp.full((total_rows, LANES), -1e30, jnp.float32)
    wide_total[...] = jnp.zeros((total_rows, LANES), jnp.float32)
    wide_positive[...] = jnp.zeros((total_rows, LANES), jnp.float32)

    def is_positive(start):
        ids = start + lax.broadcasted_iota(jnp.int32, (total_rows, LANES), 1)
        return ids == wide_column[...]

    @pl.loop(0, total_keys // block)
    def _(step):
        at = pl.ds(pl.multiple_of(step * block, block), block)
        product = (
            lax.dot_general(
                queries[...], keys[at, :], (((1,), (1,)), ((), ())),
                preferred_element_type=jnp.float32,
            )
            * factor
        )
        scores[:, at] = product
        peak = wide_peak[...]
        positive = wide_positive[...]
        for half in range(block // LANES):
            piece = product[:, half * LANES : (half + 1) * LANES]
            peak = jnp.maximum(peak, piece)
            positive = positive + jnp.where(is_positive(step * block + half * LANES), piece, 0.0)
        wide_peak[...] = peak
        wide_positive[...] = positive

    peak = jnp.max(wide_peak[...], axis=1, keepdims=True)
    wide_peak[...] = jnp.broadcast_to(peak, (total_rows, LANES))

    @pl.loop(0, total_keys // block)
    def _(step):
        total = wide_total[...]
        for half in range(block // LANES):
            at = pl.ds(pl.multiple_of(step * block + half * LANES, LANES), LANES)
            power = jnp.exp(scores[:, at] - wide_peak[...])
            scores[:, at] = power
            total = total + power
        wide_total[...] = total

    total = jnp.sum(wide_total[...], axis=1, keepdims=True)
    positive = jnp.sum(wide_positive[...], axis=1, keepdims=True)
    for i in range(nz):
        at = slice(i * rows, (i + 1) * rows)
        stats[z, i, 0:1, :] = row_of(peak[at])
        stats[z, i, 1:2, :] = row_of(total[at])
        stats[z, i, 2:3, :] = row_of(positive[at])

    def stats_push(d, owner, target):
        at = stats.at[owner]
        return push(at, at, st_s.at[d], st_r.at[d], target, mp)

    for d in range(1, nz):
        start(stats_push(d, z, z_dev(d)))
    for d in range(1, nz):
        stats_push(d, lax.rem(z + nz - d, nz), me).wait_recv()

    top = stats[0, :, 0, :]
    for i in range(1, nz):
        top = jnp.maximum(top, stats[i, :, 0, :])
    whole = jnp.zeros_like(top)
    found = jnp.zeros_like(top)
    for i in range(nz):
        whole = whole + stats[i, :, 1, :] * jnp.exp(stats[i, :, 0, :] - top)
        found = found + stats[i, :, 2, :]
    log_rows = top + jnp.log(jnp.maximum(whole, 1e-30))
    losses = log_rows - found
    loss_line = jnp.zeros((1, LANES), jnp.float32)
    for i in range(nz):
        loss_line = loss_line + jnp.where(z == i, losses[i : i + 1, :], 0.0)
    loss_ref[...] = jnp.broadcast_to(loss_line, loss_ref.shape)
    log_total = jnp.concatenate(
        [column_of(log_rows[i : i + 1, :], 0, rows) for i in range(nz)], axis=0
    )

    wide_total[...] = jnp.broadcast_to(jnp.exp(peak - log_total), (total_rows, LANES))

    @pl.loop(0, total_keys // block)
    def _(step):
        for half in range(block // LANES):
            start_at = pl.multiple_of(step * block + half * LANES, LANES)
            at = pl.ds(start_at, LANES)
            probs[:, at] = (
                scores[:, at] * wide_total[...] - jnp.where(is_positive(start_at), 1.0, 0.0)
            ).astype(jnp.bfloat16)

    n_blocks = width // block

    def grad_push(way, c, owner, target):
        return push(
            partial.at[c, z_rows(owner), :], arrived.at[way, c, owner],
            g_s.at[way, c, owner], g_r.at[way, c, owner], target * GROUP + slot, mp,
        )

    for c in range(n_blocks):
        partial[c] = jnp.dot(
            probs[...], keys[:, c * block : (c + 1) * block], preferred_element_type=jnp.float32
        ).astype(jnp.bfloat16)
        for i in range(nz - 1):
            guarded_start(z == 0, functools.partial(grad_push, 0, c, nz - 1 - i, 1))
            guarded_start(z == nz - 1, functools.partial(grad_push, 1, c, i, nz - 2))

    def relay(condition, way, c, owner, target):
        @pl.when(condition)
        def _():
            grad_push(way, c, owner, z).wait_recv()
            at = z_rows(owner)
            partial[c, at, :] = (
                partial[c, at, :].astype(jnp.float32)
                + arrived[way, c, owner].astype(jnp.float32)
            ).astype(jnp.bfloat16)

        guarded_start(condition, functools.partial(grad_push, way, c, owner, target))

    for c in range(n_blocks):
        for i in range(nz - 1):
            owner = nz - 1 - i
            relay(has_left & (z < owner), 0, c, owner, z + 1)
            relay(has_right & (z > i), 1, c, i, z - 1)

    scaled = []
    inner = jnp.zeros((rows, 1), jnp.float32)
    for c in range(n_blocks):
        for way, there in ((0, has_left), (1, has_right)):
            @pl.when(there)
            def _():
                grad_push(way, c, z, z).wait_recv()

            @pl.when(jnp.logical_not(there))
            def _():
                arrived[way, c, z] = jnp.zeros((rows, block), jnp.bfloat16)

        summed = partial[c, own_rows, :].astype(jnp.float32)
        summed = summed + arrived[0, c, z].astype(jnp.float32)
        summed = summed + arrived[1, c, z].astype(jnp.float32)
        at = slice(c * block, (c + 1) * block)
        block_scaled = gain_ref[:, at] * (summed * (16.0 * factor))
        scaled.append(block_scaled)
        inner = inner + jnp.sum(block_scaled * hidden[:, at], axis=1, keepdims=True)
    inner = inverse_rms * inverse_rms * inverse_rms * inner / width
    hidden_grad = jnp.concatenate(
        [
            (inverse_rms * scaled[c] - hidden[:, c * block : (c + 1) * block] * inner).astype(
                jnp.bfloat16
            )
            for c in range(n_blocks)
        ],
        axis=1,
    )
    result = jnp.zeros((rows, width), jnp.float32)
    for m in range(n_mp):
        result = result + lax.dot_general(
            hidden_grad[:, m * part_width : (m + 1) * part_width], weights_in[m],
            (((1,), (1,)), ((), ())), preferred_element_type=jnp.float32,
        )
    grad_ref[...] = result.astype(jnp.bfloat16)
    for copy in sends:
        copy.wait_send()
    for condition, make in guarded:

        @pl.when(condition)
        def _(make=make):
            make().wait_send()

    next_out.wait()


def finish_kernel(
    loss_in, grad_in, next_in, loss_ref, grad_ref, next_ref, grad_held, next_held, sem_in, sem_out
):
    pieces = [(grad_in, grad_held, grad_ref, slice(None))]
    count = next_in.shape[0] // 4
    pieces += [
        (next_in, next_held, next_ref, pl.ds(i * count, count)) for i in range(4)
    ]
    loads, stores = [], []
    for i, (source, held, target, at) in enumerate(pieces):
        loads.append(pltpu.make_async_copy(source.at[at], held.at[at], sem_in.at[i]))
        stores.append(pltpu.make_async_copy(held.at[at], target.at[at], sem_out.at[i]))
    for load in loads:
        load.start()
    loss_ref[...] = loss_in[0:1, 0 : loss_ref.shape[1]]
    for load, store in zip(loads, stores):
        load.wait()
        store.start()
    for store in stores:
        store.wait()


def shards(n_queue, n_mp, speech, weight, norm_gain, queue_keys, new_keys, pointer, positives):
    rows, width = speech.shape
    key_count = queue_keys.shape[0]
    nz = n_queue // GROUP
    vmem = pl.BlockSpec(memory_space=pltpu.VMEM)
    anywhere = pl.BlockSpec(memory_space=pl.ANY)
    dma = pltpu.SemaphoreType.DMA
    bf16, f32 = jnp.bfloat16, jnp.float32
    scratch = [
        pltpu.VMEM((rows, width), bf16),
        pltpu.VMEM(new_keys.shape, bf16),
        pltpu.VMEM((key_count, width), bf16),
        pltpu.VMEM((GROUP * key_count, width), bf16),
        pltpu.VMEM((n_mp, width, width // n_mp), bf16),
        pltpu.VMEM((nz * rows, width), bf16),
        pltpu.VMEM((nz, 8, LANES), jnp.int32),
        pltpu.VMEM((nz * rows, GROUP * key_count), f32),
        pltpu.VMEM((nz * rows, GROUP * key_count), bf16),
        pltpu.VMEM((rows, width), f32),
        pltpu.VMEM((width // 256, nz * rows, 256), bf16),
        pltpu.VMEM((2, width // 256, nz, rows, 256), bf16),
        pltpu.VMEM((nz, nz, 8, LANES), f32),
        pltpu.VMEM((nz * rows, LANES), f32),
        pltpu.VMEM((nz * rows, LANES), f32),
        pltpu.VMEM((nz * rows, LANES), f32),
        pltpu.VMEM((nz * rows, LANES), jnp.int32),
        dma((5,)),
    ]
    scratch += [dma((n_mp, WEIGHT_CHUNKS))] * 10
    scratch += [dma((1,))] * 2 + [dma((KEY_CHUNKS,))] * 2 + [dma((n_mp, KEY_CHUNKS))] * 2
    scratch += [dma((KEY_CHUNKS,))] * 2 + [dma((n_mp, KEY_CHUNKS))] * 2
    scratch += [dma((2, nz, 2))] * 2 + [dma((nz,))] * 4 + [dma((2, width // 256, nz))] * 2
    loss, grad, queue_next = pl.pallas_call(
        functools.partial(step_kernel, n_queue, n_mp),
        out_shape=(
            jax.ShapeDtypeStruct((8, LANES), f32),
            jax.ShapeDtypeStruct((rows, width), bf16),
            jax.ShapeDtypeStruct((key_count, width), bf16),
        ),
        in_specs=[anywhere, anywhere, vmem, anywhere, anywhere, pl.BlockSpec(memory_space=pltpu.SMEM), vmem],
        out_specs=(vmem, vmem, anywhere),
        scratch_shapes=scratch,
        compiler_params=pltpu.CompilerParams(
            collective_id=0, has_side_effects=True, vmem_limit_bytes=63 * 1024 * 1024
        ),
        name="contrast_step",
    )(speech, weight, norm_gain[None, :], queue_keys, new_keys, pointer, positives[None, :])
    loss, grad, queue_next = pl.pallas_call(
        finish_kernel,
        out_shape=(
            jax.ShapeDtypeStruct((1, rows), f32),
            jax.ShapeDtypeStruct((rows, width), bf16),
            jax.ShapeDtypeStruct((key_count, width), bf16),
        ),
        in_specs=[vmem, anywhere, anywhere],
        out_specs=(vmem, anywhere, anywhere),
        scratch_shapes=[
            pltpu.VMEM((rows, width), bf16),
            pltpu.VMEM((key_count, width), bf16),
            dma((5,)),
            dma((5,)),
        ],
        compiler_params=pltpu.CompilerParams(vmem_limit_bytes=63 * 1024 * 1024),
        name="hand_out",
    )(loss, grad, queue_next)
    return loss[0], grad, queue_next


def solution(mesh):
    n_queue, n_mp = mesh.shape["queue"], mesh.shape["mp"]
    return jax.shard_map(
        functools.partial(shards, n_queue, n_mp),
        mesh=mesh,
        in_specs=(
            P(("queue", "mp"), None),
            P(None, "mp"),
            P(),
            P("queue", None),
            P(),
            P(),
            P(("queue", "mp")),
        ),
        out_specs=(P(("queue", "mp")), P(("queue", "mp"), None), P("queue", None)),
        check_vma=False,
    )
```

```python
import functools
import math

import jax
import jax.numpy as jnp
from jax import lax
from jax.experimental import pallas as pl
from jax.experimental.pallas import tpu as pltpu
from jax.sharding import PartitionSpec as P

MESH = pl.DeviceIdType.MESH
GROUP = 4
WEIGHT_CHUNKS = 4
KEY_CHUNKS = 6
LANES = 128


def column_of(tile, row, count):
    line = jnp.broadcast_to(tile[row : row + 1, :], (LANES, LANES))
    eye = lax.broadcasted_iota(jnp.int32, (LANES, LANES), 0) == lax.broadcasted_iota(
        jnp.int32, (LANES, LANES), 1
    )
    return jnp.sum(jnp.where(eye, line, jnp.zeros_like(line)), axis=1, keepdims=True)[:count]


def row_of(column):
    count = column.shape[0]
    wide = jnp.broadcast_to(column, (count, LANES))
    eye = lax.broadcasted_iota(jnp.int32, (count, LANES), 0) == lax.broadcasted_iota(
        jnp.int32, (count, LANES), 1
    )
    return jnp.sum(jnp.where(eye, wide, jnp.zeros_like(wide)), axis=0, keepdims=True)


def step_kernel(
    n_queue,
    n_mp,
    speech_hbm,
    weight_ref,
    gain_ref,
    keys_ref,
    new_hbm,
    pointer_ref,
    positives_ref,
    loss_ref,
    grad_ref,
    next_ref,
    speech_ref,
    new_ref,
    next_rows,
    keys,
    weights_in,
    queries,
    columns,
    scores,
    probs,
    hidden,
    partial,
    arrived,
    relay_in,
    stats,
    wide_peak,
    wide_total,
    wide_positive,
    wide_column,
    local_sem,
    wy_s, wy_r, wx_s, wx_r, wcy_s, wcy_r, wcx_s, wcx_r, wco_s, wco_r,
    kc_s, kc_r, kx_s, kx_r, ky_s, ky_r, kcx_s, kcx_r, kcy_s, kcy_r,
    q_s, q_r, p_s, p_r, st_s, st_r, g_s, g_r, r_r,
):
    rows, width = speech_ref.shape
    key_count = keys_ref.shape[0]
    nz = n_queue // GROUP
    me = lax.axis_index("queue")
    mp = lax.axis_index("mp")
    z = me // GROUP
    slot = me % GROUP
    x = slot // 2
    core = slot % 2
    core_peer = me + 1 - 2 * core
    x_peer = me + 2 - 4 * x
    core_slot = slot + 1 - 2 * core
    x_slot = slot + 2 - 4 * x
    diag_slot = core_slot + 2 - 4 * x

    def z_dev(distance):
        return lax.rem(z + distance, nz) * GROUP + slot

    def mp_dev(distance):
        return lax.rem(mp + distance, n_mp)

    def push(src, dst, send, recv, queue, mp_index):
        return pltpu.make_async_remote_copy(
            src_ref=src, dst_ref=dst, send_sem=send, recv_sem=recv,
            device_id=(queue, mp_index), device_id_type=MESH,
        )

    barrier = pltpu.get_barrier_semaphore()
    peers = [(core_peer, mp), (x_peer, mp)]
    peers += [(me, mp_dev(d)) for d in range(1, n_mp)]
    peers += [(z_dev(d), mp) for d in range(1, nz)]
    for peer in peers:
        pl.semaphore_signal(barrier, inc=1, device_id=peer, device_id_type=MESH)

    def key_rows(which, start, count):
        return keys.at[pl.ds(pl.multiple_of(which * key_count + start, 16), count), :]

    own_keys = pltpu.make_async_copy(keys_ref, key_rows(slot, 0, key_count), local_sem.at[0])
    own_weight = pltpu.make_async_copy(weight_ref, weights_in.at[mp], local_sem.at[1])
    own_speech = pltpu.make_async_copy(speech_hbm, speech_ref, local_sem.at[2])
    own_new = pltpu.make_async_copy(new_hbm, new_ref, local_sem.at[3])
    own_weight.start()
    own_speech.start()
    own_keys.start()
    own_new.start()
    pl.semaphore_wait(barrier, len(peers))

    sends = []
    guarded = []

    def start(copy):
        copy.start()
        sends.append(copy)

    w_count = width // GROUP // WEIGHT_CHUNKS

    def w_push(dist, quarter, j, shard, sems, queue, mp_index, src=None):
        at = pl.ds(pl.multiple_of(quarter * (width // GROUP) + j * w_count, 16), w_count)
        dst = weights_in.at[shard, at, :]
        return push(
            dst if src is None else src.at[at, :], dst,
            sems[0].at[dist, j], sems[1].at[dist, j], queue, mp_index,
        )

    for j in range(WEIGHT_CHUNKS):
        for d in range(1, n_mp):
            start(w_push(d, slot, j, mp, (wy_s, wy_r), me, mp_dev(d), weight_ref))

    part = key_count // n_mp
    k_count = part // KEY_CHUNKS

    def k_start(shard, j):
        return shard * part + j * k_count

    def key_x(j):
        at = k_start(mp, j)
        return push(
            keys_ref.at[pl.ds(pl.multiple_of(at, 16), k_count), :], key_rows(slot, at, k_count),
            kx_s.at[j], kx_r.at[j], x_peer, mp,
        )

    def key_forward(shard, j, send, recv, queue, mp_index, which=x_slot):
        at = key_rows(which, k_start(shard, j), k_count)
        return push(at, at, send, recv, queue, mp_index)

    def key_arrive_x(j):
        key_forward(mp, j, kx_s.at[j], kx_r.at[j], x_peer, mp).wait_recv()
        for d in range(1, n_mp):
            start(key_forward(mp, j, ky_s.at[d, j], ky_r.at[d, j], me, mp_dev(d)))
        start(key_forward(mp, j, kcx_s.at[j], kcx_r.at[j], core_peer, mp))

    def key_arrive_y(j):
        for d in range(1, n_mp):
            shard = mp_dev(n_mp - d)
            key_forward(shard, j, ky_s.at[d, j], ky_r.at[d, j], me, mp).wait_recv()
            start(key_forward(shard, j, kcy_s.at[d, j], kcy_r.at[d, j], core_peer, mp))

    start(key_x(0))
    start(push(keys_ref, key_rows(slot, 0, key_count), kc_s.at[0], kc_r.at[0], core_peer, mp))

    for j in range(WEIGHT_CHUNKS):
        for d in range(1, n_mp):
            shard = mp_dev(n_mp - d)
            w_push(d, slot, j, shard, (wy_s, wy_r), me, mp).wait_recv()
            start(w_push(d, slot, j, shard, (wx_s, wx_r), x_peer, mp))
            start(w_push(d, slot, j, shard, (wcy_s, wcy_r), core_peer, mp))
    for j in range(1, KEY_CHUNKS):
        start(key_x(j))
    for j in range(WEIGHT_CHUNKS):
        for d in range(1, n_mp):
            shard = mp_dev(n_mp - d)
            w_push(d, x_slot, j, shard, (wx_s, wx_r), x_peer, mp).wait_recv()
            start(w_push(d, x_slot, j, shard, (wcx_s, wcx_r), core_peer, mp))
    key_arrive_x(0)
    own_speech.wait()
    own_weight.wait()
    for j in range(WEIGHT_CHUNKS):
        for d in range(1, n_mp):
            shard = mp_dev(n_mp - d)
            w_push(d, core_slot, j, shard, (wcy_s, wcy_r), core_peer, mp).wait_recv()
            w_push(d, diag_slot, j, shard, (wcx_s, wcx_r), core_peer, mp).wait_recv()

    part_width = width // n_mp
    for m in range(n_mp):
        hidden[:, m * part_width : (m + 1) * part_width] = jnp.dot(
            speech_ref[...], weights_in[m], preferred_element_type=jnp.float32
        )
    encoded = hidden[...]
    inverse_rms = lax.rsqrt(jnp.mean(encoded * encoded, axis=1, keepdims=True) + 1e-06)
    own_rows = pl.ds(pl.multiple_of(z * rows, 16), rows)
    queries[own_rows, :] = (encoded * inverse_rms * gain_ref[...]).astype(jnp.bfloat16)
    columns[z, 0:1, 0:rows] = positives_ref[...]

    def z_rows(index):
        return pl.ds(pl.multiple_of(index * rows, 16), rows)

    has_left, has_right = z > 0, z < nz - 1

    def guarded_start(condition, make):
        @pl.when(condition)
        def _():
            make().start()

        guarded.append((condition, make))

    relayed = nz > 2

    def query_push(owner, target):
        at = queries.at[z_rows(owner), :]
        return push(at, at, q_s.at[owner, target], q_r.at[owner], target * GROUP + slot, mp)

    def column_push(d, owner, target):
        at = columns.at[owner]
        return push(at, at, p_s.at[d], p_r.at[d], target, mp)

    def between_ends(source, target):
        if not relayed:
            return source != source
        low = (source == 0) & (target == nz - 1)
        return low | ((source == nz - 1) & (target == 0))

    for distance in range(nz - 1, 0, -1):
        for target in (z + distance, z - distance):
            there = (target >= 0) & (target < nz)
            guarded_start(
                there & jnp.logical_not(between_ends(z, target)),
                functools.partial(query_push, z, target),
            )
    for d in range(1, nz):
        start(column_push(d, z, z_dev(d)))

    def query_relay():
        for owner, via, target in ((0, nz - 2, nz - 1), (nz - 1, 1, 0)):

            @pl.when(z == via)
            def _():
                query_push(owner, via).wait_recv()

            guarded_start(z == via, functools.partial(query_push, owner, target))

    def take_rows(step):
        block = key_count // 3
        at = pl.ds(step * block, block)
        length = key_count * n_queue
        ids = me * key_count + step * block + lax.broadcasted_iota(jnp.int32, (block, 1), 0)
        offsets = ids - pointer_ref[0]
        offsets = jnp.where(offsets < 0, offsets + length, offsets)
        count = new_ref.shape[0]
        chosen = lax.broadcasted_iota(jnp.int32, (block, count), 1) == offsets
        taken = jnp.dot(
            jnp.where(chosen, 1.0, 0.0).astype(jnp.bfloat16), new_ref[...],
            preferred_element_type=jnp.float32,
        )
        held = keys[pl.ds(pl.multiple_of(slot * key_count + step * block, 16), block), :]
        next_rows[at, :] = jnp.where(offsets < count, taken, held.astype(jnp.float32)).astype(
            jnp.bfloat16
        )

    own_keys.wait()
    for j in range(1, KEY_CHUNKS):
        key_arrive_x(j)
        if j == 1:
            own_new.wait()
            for step in range(3):
                take_rows(step)
            next_out = pltpu.make_async_copy(next_rows, next_ref, local_sem.at[4])
            next_out.start()
        if j > 1:
            key_arrive_y(j - 2)
        if j == KEY_CHUNKS - 2 and relayed:
            query_relay()
    for j in range(KEY_CHUNKS - 2, KEY_CHUNKS):
        key_arrive_y(j)
    push(
        keys_ref, key_rows(core_slot, 0, key_count), kc_s.at[0], kc_r.at[0], core_peer, mp
    ).wait_recv()
    for j in range(KEY_CHUNKS):
        key_forward(mp, j, kcx_s.at[j], kcx_r.at[j], core_peer, mp, diag_slot).wait_recv()
        for d in range(1, n_mp):
            shard = mp_dev(n_mp - d)
            key_forward(
                shard, j, kcy_s.at[d, j], kcy_r.at[d, j], core_peer, mp, diag_slot
            ).wait_recv()

    for d in range(1, nz):
        source = lax.rem(z + nz - d, nz)
        column_push(d, source, me).wait_recv()
    for owner in range(nz):
        waiting = z != owner
        if relayed and owner in (0, nz - 1):
            waiting = waiting & (z != (nz - 2 if owner == 0 else 1))

        @pl.when(waiting)
        def _():
            query_push(owner, z).wait_recv()


    factor = 2.0 / math.sqrt(width)
    total_rows = nz * rows
    total_keys = GROUP * key_count
    block = 256
    for i in range(nz):
        wide_column[i * rows : (i + 1) * rows, :] = jnp.broadcast_to(
            column_of(columns[i], 0, rows) - z * total_keys, (rows, LANES)
        )
    wide_peak[...] = jnp.full((total_rows, LANES), -1e30, jnp.float32)
    wide_total[...] = jnp.zeros((total_rows, LANES), jnp.float32)
    wide_positive[...] = jnp.zeros((total_rows, LANES), jnp.float32)

    def is_positive(start):
        ids = start + lax.broadcasted_iota(jnp.int32, (total_rows, LANES), 1)
        return ids == wide_column[...]

    @pl.loop(0, total_keys // block)
    def _(step):
        at = pl.ds(pl.multiple_of(step * block, block), block)
        product = (
            lax.dot_general(
                queries[...], keys[at, :], (((1,), (1,)), ((), ())),
                preferred_element_type=jnp.float32,
            )
            * factor
        )
        scores[:, at] = product
        peak = wide_peak[...]
        positive = wide_positive[...]
        for half in range(block // LANES):
            piece = product[:, half * LANES : (half + 1) * LANES]
            peak = jnp.maximum(peak, piece)
            positive = positive + jnp.where(is_positive(step * block + half * LANES), piece, 0.0)
        wide_peak[...] = peak
        wide_positive[...] = positive

    peak = jnp.max(wide_peak[...], axis=1, keepdims=True)
    wide_peak[...] = jnp.broadcast_to(peak, (total_rows, LANES))

    @pl.loop(0, total_keys // block)
    def _(step):
        total = wide_total[...]
        for half in range(block // LANES):
            at = pl.ds(pl.multiple_of(step * block + half * LANES, LANES), LANES)
            power = jnp.exp(scores[:, at] - wide_peak[...])
            scores[:, at] = power
            total = total + power
        wide_total[...] = total

    total = jnp.sum(wide_total[...], axis=1, keepdims=True)
    positive = jnp.sum(wide_positive[...], axis=1, keepdims=True)
    for i in range(nz):
        at = slice(i * rows, (i + 1) * rows)
        stats[z, i, 0:1, :] = row_of(peak[at])
        stats[z, i, 1:2, :] = row_of(total[at])
        stats[z, i, 2:3, :] = row_of(positive[at])

    def stats_push(d, owner, target):
        at = stats.at[owner]
        return push(at, at, st_s.at[d], st_r.at[d], target, mp)

    for d in range(1, nz):
        start(stats_push(d, z, z_dev(d)))
    for d in range(1, nz):
        stats_push(d, lax.rem(z + nz - d, nz), me).wait_recv()

    top = stats[0, :, 0, :]
    for i in range(1, nz):
        top = jnp.maximum(top, stats[i, :, 0, :])
    whole = jnp.zeros_like(top)
    found = jnp.zeros_like(top)
    for i in range(nz):
        whole = whole + stats[i, :, 1, :] * jnp.exp(stats[i, :, 0, :] - top)
        found = found + stats[i, :, 2, :]
    log_rows = top + jnp.log(jnp.maximum(whole, 1e-30))
    losses = log_rows - found
    loss_line = jnp.zeros((1, LANES), jnp.float32)
    for i in range(nz):
        loss_line = loss_line + jnp.where(z == i, losses[i : i + 1, :], 0.0)
    loss_ref[...] = jnp.broadcast_to(loss_line, loss_ref.shape)
    log_total = jnp.concatenate(
        [column_of(log_rows[i : i + 1, :], 0, rows) for i in range(nz)], axis=0
    )

    wide_total[...] = jnp.broadcast_to(jnp.exp(peak - log_total), (total_rows, LANES))

    @pl.loop(0, total_keys // block)
    def _(step):
        for half in range(block // LANES):
            start_at = pl.multiple_of(step * block + half * LANES, LANES)
            at = pl.ds(start_at, LANES)
            probs[:, at] = (
                scores[:, at] * wide_total[...] - jnp.where(is_positive(start_at), 1.0, 0.0)
            ).astype(jnp.bfloat16)

    n_blocks = width // block

    def grad_push(c, owner, source, target):
        return push(
            partial.at[c, z_rows(owner), :], arrived.at[c, source],
            g_s.at[c, owner], g_r.at[c, source], target * GROUP + slot, mp,
        )

    def grad_relay(c):
        for source, via, owner in ((0, 1, nz - 1), (nz - 1, nz - 2, 0)):

            @pl.when(z == via)
            def _():
                grad_relay_push(c, owner, via).wait_recv()
                at = slice(owner * rows, (owner + 1) * rows)
                partial[c, at, :] = (
                    partial[c, at, :].astype(jnp.float32)
                    + relay_in[c].astype(jnp.float32)
                ).astype(jnp.bfloat16)

            guarded_start(z == via, functools.partial(grad_push, c, owner, via, owner))

    def grad_relay_push(c, owner, target):
        return push(
            partial.at[c, z_rows(owner), :], relay_in.at[c],
            g_s.at[c, owner], r_r.at[c], target * GROUP + slot, mp,
        )

    for c in range(n_blocks):
        partial[c] = jnp.dot(
            probs[...], keys[:, c * block : (c + 1) * block], preferred_element_type=jnp.float32
        ).astype(jnp.bfloat16)
        if relayed:
            guarded_start(z == 0, functools.partial(grad_relay_push, c, nz - 1, 1))
            guarded_start(z == nz - 1, functools.partial(grad_relay_push, c, 0, nz - 2))
        for distance in range(nz - 1, 0, -1):
            for owner in (z + distance, z - distance):
                there = (owner >= 0) & (owner < nz) & jnp.logical_not(between_ends(z, owner))
                if relayed:
                    there = there & jnp.logical_not((z == 1) & (owner == nz - 1))
                    there = there & jnp.logical_not((z == nz - 2) & (owner == 0))
                guarded_start(there, functools.partial(grad_push, c, owner, z, owner))
        if relayed and c > 0:
            grad_relay(c - 1)
    if relayed:
        grad_relay(n_blocks - 1)

    scaled = []
    inner = jnp.zeros((rows, 1), jnp.float32)
    for c in range(n_blocks):
        for source in range(nz):
            absent = (z == source) | between_ends(z, jnp.int32(source))

            @pl.when(jnp.logical_not(absent))
            def _():
                grad_push(c, z, source, z).wait_recv()

            @pl.when(absent)
            def _():
                arrived[c, source] = jnp.zeros((rows, block), jnp.bfloat16)

        summed = partial[c, own_rows, :].astype(jnp.float32)
        for source in range(nz):
            summed = summed + arrived[c, source].astype(jnp.float32)
        at = slice(c * block, (c + 1) * block)
        block_scaled = gain_ref[:, at] * (summed * (16.0 * factor))
        scaled.append(block_scaled)
        inner = inner + jnp.sum(block_scaled * hidden[:, at], axis=1, keepdims=True)
    inner = inverse_rms * inverse_rms * inverse_rms * inner / width
    hidden_grad = jnp.concatenate(
        [
            (inverse_rms * scaled[c] - hidden[:, c * block : (c + 1) * block] * inner).astype(
                jnp.bfloat16
            )
            for c in range(n_blocks)
        ],
        axis=1,
    )
    result = jnp.zeros((rows, width), jnp.float32)
    for m in range(n_mp):
        result = result + lax.dot_general(
            hidden_grad[:, m * part_width : (m + 1) * part_width], weights_in[m],
            (((1,), (1,)), ((), ())), preferred_element_type=jnp.float32,
        )
    grad_ref[...] = result.astype(jnp.bfloat16)
    for copy in sends:
        copy.wait_send()
    for condition, make in guarded:

        @pl.when(condition)
        def _(make=make):
            make().wait_send()

    next_out.wait()


def finish_kernel(
    loss_in, grad_in, next_in, loss_ref, grad_ref, next_ref, grad_held, next_held, sem_in, sem_out
):
    pieces = [(grad_in, grad_held, grad_ref, slice(None))]
    count = next_in.shape[0] // 4
    pieces += [
        (next_in, next_held, next_ref, pl.ds(i * count, count)) for i in range(4)
    ]
    loads, stores = [], []
    for i, (source, held, target, at) in enumerate(pieces):
        loads.append(pltpu.make_async_copy(source.at[at], held.at[at], sem_in.at[i]))
        stores.append(pltpu.make_async_copy(held.at[at], target.at[at], sem_out.at[i]))
    for load in loads:
        load.start()
    loss_ref[...] = loss_in[0:1, 0 : loss_ref.shape[1]]
    for load, store in zip(loads, stores):
        load.wait()
        store.start()
    for store in stores:
        store.wait()


def shards(n_queue, n_mp, speech, weight, norm_gain, queue_keys, new_keys, pointer, positives):
    rows, width = speech.shape
    key_count = queue_keys.shape[0]
    nz = n_queue // GROUP
    vmem = pl.BlockSpec(memory_space=pltpu.VMEM)
    anywhere = pl.BlockSpec(memory_space=pl.ANY)
    dma = pltpu.SemaphoreType.DMA
    bf16, f32 = jnp.bfloat16, jnp.float32
    scratch = [
        pltpu.VMEM((rows, width), bf16),
        pltpu.VMEM(new_keys.shape, bf16),
        pltpu.VMEM((key_count, width), bf16),
        pltpu.VMEM((GROUP * key_count, width), bf16),
        pltpu.VMEM((n_mp, width, width // n_mp), bf16),
        pltpu.VMEM((nz * rows, width), bf16),
        pltpu.VMEM((nz, 8, LANES), jnp.int32),
        pltpu.VMEM((nz * rows, GROUP * key_count), f32),
        pltpu.VMEM((nz * rows, GROUP * key_count), bf16),
        pltpu.VMEM((rows, width), f32),
        pltpu.VMEM((width // 256, nz * rows, 256), bf16),
        pltpu.VMEM((width // 256, nz, rows, 256), bf16),
        pltpu.VMEM((width // 256, rows, 256), bf16),
        pltpu.VMEM((nz, nz, 8, LANES), f32),
        pltpu.VMEM((nz * rows, LANES), f32),
        pltpu.VMEM((nz * rows, LANES), f32),
        pltpu.VMEM((nz * rows, LANES), f32),
        pltpu.VMEM((nz * rows, LANES), jnp.int32),
        dma((5,)),
    ]
    scratch += [dma((n_mp, WEIGHT_CHUNKS))] * 10
    scratch += [dma((1,))] * 2 + [dma((KEY_CHUNKS,))] * 2 + [dma((n_mp, KEY_CHUNKS))] * 2
    scratch += [dma((KEY_CHUNKS,))] * 2 + [dma((n_mp, KEY_CHUNKS))] * 2
    scratch += [dma((nz, nz)), dma((nz,))] + [dma((nz,))] * 4
    scratch += [dma((width // 256, nz))] * 2 + [dma((width // 256,))]
    loss, grad, queue_next = pl.pallas_call(
        functools.partial(step_kernel, n_queue, n_mp),
        out_shape=(
            jax.ShapeDtypeStruct((8, LANES), f32),
            jax.ShapeDtypeStruct((rows, width), bf16),
            jax.ShapeDtypeStruct((key_count, width), bf16),
        ),
        in_specs=[anywhere, anywhere, vmem, anywhere, anywhere, pl.BlockSpec(memory_space=pltpu.SMEM), vmem],
        out_specs=(vmem, vmem, anywhere),
        scratch_shapes=scratch,
        compiler_params=pltpu.CompilerParams(
            collective_id=0, has_side_effects=True, vmem_limit_bytes=63 * 1024 * 1024
        ),
        name="contrast_step",
    )(speech, weight, norm_gain[None, :], queue_keys, new_keys, pointer, positives[None, :])
    loss, grad, queue_next = pl.pallas_call(
        finish_kernel,
        out_shape=(
            jax.ShapeDtypeStruct((1, rows), f32),
            jax.ShapeDtypeStruct((rows, width), bf16),
            jax.ShapeDtypeStruct((key_count, width), bf16),
        ),
        in_specs=[vmem, anywhere, anywhere],
        out_specs=(vmem, anywhere, anywhere),
        scratch_shapes=[
            pltpu.VMEM((rows, width), bf16),
            pltpu.VMEM((key_count, width), bf16),
            dma((5,)),
            dma((5,)),
        ],
        compiler_params=pltpu.CompilerParams(vmem_limit_bytes=63 * 1024 * 1024),
        name="hand_out",
    )(loss, grad, queue_next)
    return loss[0], grad, queue_next


def solution(mesh):
    n_queue, n_mp = mesh.shape["queue"], mesh.shape["mp"]
    return jax.shard_map(
        functools.partial(shards, n_queue, n_mp),
        mesh=mesh,
        in_specs=(
            P(("queue", "mp"), None),
            P(None, "mp"),
            P(),
            P("queue", None),
            P(),
            P(),
            P(("queue", "mp")),
        ),
        out_specs=(P(("queue", "mp")), P(("queue", "mp"), None), P("queue", None)),
        check_vma=False,
    )
```

```python
import functools
import math

import jax
import jax.numpy as jnp
from jax import lax
from jax.experimental import pallas as pl
from jax.experimental.pallas import tpu as pltpu
from jax.sharding import PartitionSpec as P

MESH = pl.DeviceIdType.MESH
GROUP = 4
WEIGHT_CHUNKS = 4
KEY_CHUNKS = 6
HALVES = 2
LANES = 128


def column_of(tile, row, count):
    line = jnp.broadcast_to(tile[row : row + 1, :], (LANES, LANES))
    eye = lax.broadcasted_iota(jnp.int32, (LANES, LANES), 0) == lax.broadcasted_iota(
        jnp.int32, (LANES, LANES), 1
    )
    return jnp.sum(jnp.where(eye, line, jnp.zeros_like(line)), axis=1, keepdims=True)[:count]


def row_of(column):
    count = column.shape[0]
    wide = jnp.broadcast_to(column, (count, LANES))
    eye = lax.broadcasted_iota(jnp.int32, (count, LANES), 0) == lax.broadcasted_iota(
        jnp.int32, (count, LANES), 1
    )
    return jnp.sum(jnp.where(eye, wide, jnp.zeros_like(wide)), axis=0, keepdims=True)


def step_kernel(
    n_queue,
    n_mp,
    speech_hbm,
    weight_ref,
    gain_ref,
    keys_ref,
    new_hbm,
    pointer_ref,
    positives_ref,
    loss_ref,
    grad_ref,
    next_ref,
    speech_ref,
    new_ref,
    keys,
    weights_in,
    queries,
    columns,
    scores,
    probs,
    hidden,
    partial,
    arrived,
    relay_in,
    stats,
    wide_peak,
    wide_total,
    wide_positive,
    wide_column,
    local_sem,
    wy_s, wy_r, wx_s, wx_r, wcy_s, wcy_r, wcx_s, wcx_r, wco_s, wco_r,
    kc_s, kc_r, kx_s, kx_r, ky_s, ky_r, kcx_s, kcx_r, kcy_s, kcy_r,
    q_s, q_r, p_s, p_r, st_s, st_r, g_s, g_r, r_r,
):
    rows, width = speech_ref.shape
    key_count = keys_ref.shape[0]
    nz = n_queue // GROUP
    me = lax.axis_index("queue")
    mp = lax.axis_index("mp")
    z = me // GROUP
    slot = me % GROUP
    x = slot // 2
    core = slot % 2
    core_peer = me + 1 - 2 * core
    x_peer = me + 2 - 4 * x
    core_slot = slot + 1 - 2 * core
    x_slot = slot + 2 - 4 * x
    diag_slot = core_slot + 2 - 4 * x

    def z_dev(distance):
        return lax.rem(z + distance, nz) * GROUP + slot

    def mp_dev(distance):
        return lax.rem(mp + distance, n_mp)

    def push(src, dst, send, recv, queue, mp_index):
        return pltpu.make_async_remote_copy(
            src_ref=src, dst_ref=dst, send_sem=send, recv_sem=recv,
            device_id=(queue, mp_index), device_id_type=MESH,
        )

    barrier = pltpu.get_barrier_semaphore()
    peers = [(core_peer, mp), (x_peer, mp)]
    peers += [(me, mp_dev(d)) for d in range(1, n_mp)]
    peers += [(z_dev(d), mp) for d in range(1, nz)]
    for peer in peers:
        pl.semaphore_signal(barrier, inc=1, device_id=peer, device_id_type=MESH)

    def key_rows(which, start, count):
        return keys.at[pl.ds(pl.multiple_of(which * key_count + start, 16), count), :]

    own_keys = pltpu.make_async_copy(keys_ref, key_rows(slot, 0, key_count), local_sem.at[0])
    own_weight = pltpu.make_async_copy(weight_ref, weights_in.at[mp], local_sem.at[1])
    own_speech = pltpu.make_async_copy(speech_hbm, speech_ref, local_sem.at[2])
    own_new = pltpu.make_async_copy(new_hbm, new_ref, local_sem.at[3])
    own_weight.start()
    own_speech.start()
    own_keys.start()
    own_new.start()
    pl.semaphore_wait(barrier, len(peers))

    sends = []
    guarded = []

    def start(copy):
        copy.start()
        sends.append(copy)

    w_count = width // GROUP // WEIGHT_CHUNKS

    def w_push(dist, quarter, j, shard, sems, queue, mp_index, src=None):
        at = pl.ds(pl.multiple_of(quarter * (width // GROUP) + j * w_count, 16), w_count)
        dst = weights_in.at[shard, at, :]
        return push(
            dst if src is None else src.at[at, :], dst,
            sems[0].at[dist, j], sems[1].at[dist, j], queue, mp_index,
        )

    for j in range(WEIGHT_CHUNKS):
        for d in range(1, n_mp):
            start(w_push(d, slot, j, mp, (wy_s, wy_r), me, mp_dev(d), weight_ref))

    part = key_count // n_mp
    k_count = part // KEY_CHUNKS

    def k_start(shard, j):
        return shard * part + j * k_count

    def key_x(j):
        at = k_start(mp, j)
        return push(
            keys_ref.at[pl.ds(pl.multiple_of(at, 16), k_count), :], key_rows(slot, at, k_count),
            kx_s.at[j], kx_r.at[j], x_peer, mp,
        )

    def key_forward(shard, j, send, recv, queue, mp_index, which=x_slot):
        at = key_rows(which, k_start(shard, j), k_count)
        return push(at, at, send, recv, queue, mp_index)

    def key_arrive_x(j):
        key_forward(mp, j, kx_s.at[j], kx_r.at[j], x_peer, mp).wait_recv()
        for d in range(1, n_mp):
            start(key_forward(mp, j, ky_s.at[d, j], ky_r.at[d, j], me, mp_dev(d)))
        start(key_forward(mp, j, kcx_s.at[j], kcx_r.at[j], core_peer, mp))

    def key_arrive_y(j):
        for d in range(1, n_mp):
            shard = mp_dev(n_mp - d)
            key_forward(shard, j, ky_s.at[d, j], ky_r.at[d, j], me, mp).wait_recv()
            start(key_forward(shard, j, kcy_s.at[d, j], kcy_r.at[d, j], core_peer, mp))

    start(key_x(0))
    start(push(keys_ref, key_rows(slot, 0, key_count), kc_s.at[0], kc_r.at[0], core_peer, mp))

    for j in range(WEIGHT_CHUNKS):
        for d in range(1, n_mp):
            shard = mp_dev(n_mp - d)
            w_push(d, slot, j, shard, (wy_s, wy_r), me, mp).wait_recv()
            start(w_push(d, slot, j, shard, (wx_s, wx_r), x_peer, mp))
            start(w_push(d, slot, j, shard, (wcy_s, wcy_r), core_peer, mp))
    for j in range(1, KEY_CHUNKS):
        start(key_x(j))
    for j in range(WEIGHT_CHUNKS):
        for d in range(1, n_mp):
            shard = mp_dev(n_mp - d)
            w_push(d, x_slot, j, shard, (wx_s, wx_r), x_peer, mp).wait_recv()
            start(w_push(d, x_slot, j, shard, (wcx_s, wcx_r), core_peer, mp))
    key_arrive_x(0)
    own_speech.wait()
    own_weight.wait()
    for j in range(WEIGHT_CHUNKS):
        for d in range(1, n_mp):
            shard = mp_dev(n_mp - d)
            w_push(d, core_slot, j, shard, (wcy_s, wcy_r), core_peer, mp).wait_recv()
            w_push(d, diag_slot, j, shard, (wcx_s, wcx_r), core_peer, mp).wait_recv()

    part_width = width // n_mp
    for m in range(n_mp):
        hidden[:, m * part_width : (m + 1) * part_width] = jnp.dot(
            speech_ref[...], weights_in[m], preferred_element_type=jnp.float32
        )
    encoded = hidden[...]
    inverse_rms = lax.rsqrt(jnp.mean(encoded * encoded, axis=1, keepdims=True) + 1e-06)
    part_rows = rows // HALVES
    normed = (encoded * inverse_rms * gain_ref[...]).astype(jnp.bfloat16)
    for h in range(HALVES):
        queries[h, pl.ds(pl.multiple_of(z * part_rows, 16), part_rows), :] = normed[
            h * part_rows : (h + 1) * part_rows
        ]
    columns[z, 0:1, 0:rows] = positives_ref[...]

    def z_rows(index):
        return pl.ds(pl.multiple_of(index * part_rows, 16), part_rows)


    def guarded_start(condition, make):
        @pl.when(condition)
        def _():
            make().start()

        guarded.append((condition, make))

    relayed = nz > 2

    def query_push(h, owner, target):
        at = queries.at[h, z_rows(owner), :]
        return push(
            at, at, q_s.at[h, owner, target], q_r.at[h, owner], target * GROUP + slot, mp
        )

    def column_push(d, owner, target):
        at = columns.at[owner]
        return push(at, at, p_s.at[d], p_r.at[d], target, mp)

    def between_ends(source, target):
        if not relayed:
            return source != source
        low = (source == 0) & (target == nz - 1)
        return low | ((source == nz - 1) & (target == 0))

    for h in range(HALVES):
        for distance in range(nz - 1, 0, -1):
            for target in (z + distance, z - distance):
                there = (target >= 0) & (target < nz)
                guarded_start(
                    there & jnp.logical_not(between_ends(z, target)),
                    functools.partial(query_push, h, z, target),
                )
    for d in range(1, nz):
        start(column_push(d, z, z_dev(d)))

    def query_relay(h):
        for owner, via, target in ((0, nz - 2, nz - 1), (nz - 1, 1, 0)):

            @pl.when(z == via)
            def _():
                query_push(h, owner, via).wait_recv()

            guarded_start(z == via, functools.partial(query_push, h, owner, target))

    def take_rows(step):
        block = key_count // 3
        at = pl.ds(step * block, block)
        length = key_count * n_queue
        ids = me * key_count + step * block + lax.broadcasted_iota(jnp.int32, (block, 1), 0)
        offsets = ids - pointer_ref[0]
        offsets = jnp.where(offsets < 0, offsets + length, offsets)
        count = new_ref.shape[0]
        chosen = lax.broadcasted_iota(jnp.int32, (block, count), 1) == offsets
        taken = jnp.dot(
            jnp.where(chosen, 1.0, 0.0).astype(jnp.bfloat16), new_ref[...],
            preferred_element_type=jnp.float32,
        )
        held = keys[pl.ds(pl.multiple_of(slot * key_count + step * block, 16), block), :]
        next_ref[at, :] = jnp.where(offsets < count, taken, held.astype(jnp.float32)).astype(
            jnp.bfloat16
        )

    own_keys.wait()
    for j in range(1, KEY_CHUNKS):
        key_arrive_x(j)
        if j == 1:
            own_new.wait()
            for step in range(3):
                take_rows(step)
        if j > 1:
            key_arrive_y(j - 2)
        if j >= KEY_CHUNKS - HALVES and relayed:
            query_relay(j - KEY_CHUNKS + HALVES)
    for j in range(KEY_CHUNKS - 2, KEY_CHUNKS):
        key_arrive_y(j)
    push(
        keys_ref, key_rows(core_slot, 0, key_count), kc_s.at[0], kc_r.at[0], core_peer, mp
    ).wait_recv()
    def diagonal_arrive():
        for j in range(KEY_CHUNKS):
            key_forward(mp, j, kcx_s.at[j], kcx_r.at[j], core_peer, mp, diag_slot).wait_recv()
            for d in range(1, n_mp):
                shard = mp_dev(n_mp - d)
                key_forward(
                    shard, j, kcy_s.at[d, j], kcy_r.at[d, j], core_peer, mp, diag_slot
                ).wait_recv()

    def queries_arrive(h):
        for owner in range(nz):
            waiting = z != owner
            if relayed and owner in (0, nz - 1):
                waiting = waiting & (z != (nz - 2 if owner == 0 else 1))

            @pl.when(waiting)
            def _():
                query_push(h, owner, z).wait_recv()

    for d in range(1, nz):
        column_push(d, lax.rem(z + nz - d, nz), me).wait_recv()

    factor = 2.0 / math.sqrt(width)
    total_rows = nz * part_rows
    total_keys = GROUP * key_count
    block = 256
    n_steps = key_count // block
    for i in range(nz):
        tile = column_of(columns[i], 0, rows) - z * total_keys
        for h in range(HALVES):
            wide_column[h, i * part_rows : (i + 1) * part_rows, :] = jnp.broadcast_to(
                tile[h * part_rows : (h + 1) * part_rows], (part_rows, LANES)
            )
    wide_peak[...] = jnp.full(wide_peak.shape, -1e30, jnp.float32)
    wide_total[...] = jnp.zeros(wide_total.shape, jnp.float32)
    wide_positive[...] = jnp.zeros(wide_positive.shape, jnp.float32)

    def is_positive(h, start):
        ids = start + lax.broadcasted_iota(jnp.int32, (total_rows, LANES), 1)
        return ids == wide_column[h]

    def score_keys(h, which):
        @pl.loop(0, n_steps)
        def _(step):
            first = pl.multiple_of(which * key_count + step * block, block)
            at = pl.ds(first, block)
            product = (
                lax.dot_general(
                    queries[h], keys[at, :], (((1,), (1,)), ((), ())),
                    preferred_element_type=jnp.float32,
                )
                * factor
            )
            scores[h, :, at] = product
            peak = wide_peak[h]
            positive = wide_positive[h]
            for half in range(block // LANES):
                piece = product[:, half * LANES : (half + 1) * LANES]
                peak = jnp.maximum(peak, piece)
                positive = positive + jnp.where(is_positive(h, first + half * LANES), piece, 0.0)
            wide_peak[h] = peak
            wide_positive[h] = positive

    def stats_push(h, d, owner, target):
        at = stats.at[h, owner]
        return push(at, at, st_s.at[h, d], st_r.at[h, d], target, mp)

    def local_stats(h):
        peak = jnp.max(wide_peak[h], axis=1, keepdims=True)
        wide_peak[h] = jnp.broadcast_to(peak, (total_rows, LANES))

        @pl.loop(0, total_keys // block)
        def _(step):
            total = wide_total[h]
            for half in range(block // LANES):
                at = pl.ds(pl.multiple_of(step * block + half * LANES, LANES), LANES)
                power = jnp.exp(scores[h, :, at] - wide_peak[h])
                scores[h, :, at] = power
                total = total + power
            wide_total[h] = total

        total = jnp.sum(wide_total[h], axis=1, keepdims=True)
        positive = jnp.sum(wide_positive[h], axis=1, keepdims=True)
        for i in range(nz):
            at = slice(i * part_rows, (i + 1) * part_rows)
            stats[h, z, i, 0:1, :] = row_of(peak[at])
            stats[h, z, i, 1:2, :] = row_of(total[at])
            stats[h, z, i, 2:3, :] = row_of(positive[at])
        for d in range(1, nz):
            start(stats_push(h, d, z, z_dev(d)))
        return peak

    def weights_of(h, peak):
        for d in range(1, nz):
            stats_push(h, d, lax.rem(z + nz - d, nz), me).wait_recv()
        top = stats[h, 0, :, 0, :]
        for i in range(1, nz):
            top = jnp.maximum(top, stats[h, i, :, 0, :])
        whole = jnp.zeros_like(top)
        found = jnp.zeros_like(top)
        for i in range(nz):
            whole = whole + stats[h, i, :, 1, :] * jnp.exp(stats[h, i, :, 0, :] - top)
            found = found + stats[h, i, :, 2, :]
        log_rows = top + jnp.log(jnp.maximum(whole, 1e-30))
        losses = log_rows - found
        loss_line = jnp.zeros((1, LANES), jnp.float32)
        for i in range(nz):
            loss_line = loss_line + jnp.where(z == i, losses[i : i + 1, :], 0.0)
        loss_ref[h : h + 1, :] = loss_line
        log_total = jnp.concatenate(
            [column_of(log_rows[i : i + 1, :], 0, part_rows) for i in range(nz)], axis=0
        )
        wide_total[h] = jnp.broadcast_to(jnp.exp(peak - log_total), (total_rows, LANES))

        @pl.loop(0, total_keys // block)
        def _(step):
            for half in range(block // LANES):
                start_at = pl.multiple_of(step * block + half * LANES, LANES)
                at = pl.ds(start_at, LANES)
                probs[:, at] = (
                    scores[h, :, at] * wide_total[h]
                    - jnp.where(is_positive(h, start_at), 1.0, 0.0)
                ).astype(jnp.bfloat16)

    for h in range(HALVES):
        queries_arrive(h)
        score_keys(h, slot)
        score_keys(h, core_slot)
    diagonal_arrive()
    peaks = []
    for h in range(HALVES):
        score_keys(h, x_slot)
        score_keys(h, diag_slot)
        peaks.append(local_stats(h))

    n_blocks = width // block

    def grad_push(h, c, owner, source, target):
        return push(
            partial.at[h, c, z_rows(owner), :], arrived.at[h, c, source],
            g_s.at[h, c, owner], g_r.at[h, c, source], target * GROUP + slot, mp,
        )

    def grad_relay_push(h, c, owner, target):
        return push(
            partial.at[h, c, z_rows(owner), :], relay_in.at[h, c],
            g_s.at[h, c, owner], r_r.at[h, c], target * GROUP + slot, mp,
        )

    def grad_relay(h, c):
        for source, via, owner in ((0, 1, nz - 1), (nz - 1, nz - 2, 0)):

            @pl.when(z == via)
            def _():
                grad_relay_push(h, c, owner, via).wait_recv()
                at = slice(owner * part_rows, (owner + 1) * part_rows)
                partial[h, c, at, :] = (
                    partial[h, c, at, :].astype(jnp.float32) + relay_in[h, c].astype(jnp.float32)
                ).astype(jnp.bfloat16)

            guarded_start(z == via, functools.partial(grad_push, h, c, owner, via, owner))

    waiting_relays = []
    for h in range(HALVES):
        weights_of(h, peaks[h])
        for c in range(n_blocks):
            partial[h, c] = jnp.dot(
                probs[...], keys[:, c * block : (c + 1) * block],
                preferred_element_type=jnp.float32,
            ).astype(jnp.bfloat16)
            if relayed:
                guarded_start(z == 0, functools.partial(grad_relay_push, h, c, nz - 1, 1))
                guarded_start(z == nz - 1, functools.partial(grad_relay_push, h, c, 0, nz - 2))
                waiting_relays.append((h, c))
            for distance in range(nz - 1, 0, -1):
                for owner in (z + distance, z - distance):
                    there = (owner >= 0) & (owner < nz) & jnp.logical_not(between_ends(z, owner))
                    if relayed:
                        there = there & jnp.logical_not((z == 1) & (owner == nz - 1))
                        there = there & jnp.logical_not((z == nz - 2) & (owner == 0))
                    guarded_start(there, functools.partial(grad_push, h, c, owner, z, owner))
            if len(waiting_relays) > 2:
                grad_relay(*waiting_relays.pop(0))
    for late in waiting_relays:
        grad_relay(*late)

    scaled = []
    inner = jnp.zeros((rows, 1), jnp.float32)
    for c in range(n_blocks):
        sums = []
        for h in range(HALVES):
            for source in range(nz):
                absent = (z == source) | between_ends(z, jnp.int32(source))

                @pl.when(jnp.logical_not(absent))
                def _():
                    grad_push(h, c, z, source, z).wait_recv()

                @pl.when(absent)
                def _():
                    arrived[h, c, source] = jnp.zeros((part_rows, block), jnp.bfloat16)

            summed = partial[h, c, z_rows(z), :].astype(jnp.float32)
            for source in range(nz):
                summed = summed + arrived[h, c, source].astype(jnp.float32)
            sums.append(summed)
        at = slice(c * block, (c + 1) * block)
        block_scaled = gain_ref[:, at] * (jnp.concatenate(sums, axis=0) * (16.0 * factor))
        scaled.append(block_scaled)
        inner = inner + jnp.sum(block_scaled * hidden[:, at], axis=1, keepdims=True)
    inner = inverse_rms * inverse_rms * inverse_rms * inner / width
    hidden_grad = jnp.concatenate(
        [
            (inverse_rms * scaled[c] - hidden[:, c * block : (c + 1) * block] * inner).astype(
                jnp.bfloat16
            )
            for c in range(n_blocks)
        ],
        axis=1,
    )
    result = jnp.zeros((rows, width), jnp.float32)
    for m in range(n_mp):
        result = result + lax.dot_general(
            hidden_grad[:, m * part_width : (m + 1) * part_width], weights_in[m],
            (((1,), (1,)), ((), ())), preferred_element_type=jnp.float32,
        )
    grad_ref[...] = result.astype(jnp.bfloat16)
    for copy in sends:
        copy.wait_send()
    for condition, make in guarded:

        @pl.when(condition)
        def _(make=make):
            make().wait_send()


def finish_kernel(
    loss_in, grad_in, next_in, loss_ref, grad_ref, next_ref, grad_held, sem_in, sem_out
):
    load = pltpu.make_async_copy(grad_in, grad_held, sem_in.at[0])
    load.start()
    count = next_in.shape[0] // 4
    stores = [pltpu.make_async_copy(grad_held, grad_ref, sem_out.at[4])]
    for i in range(4):
        at = pl.ds(i * count, count)
        stores.append(pltpu.make_async_copy(next_in.at[at], next_ref.at[at], sem_out.at[i]))
        stores[-1].start()
    count = loss_ref.shape[1] // HALVES
    for h in range(HALVES):
        loss_ref[:, h * count : (h + 1) * count] = loss_in[h : h + 1, 0:count]
    load.wait()
    stores[0].start()
    for store in stores:
        store.wait()


def shards(n_queue, n_mp, speech, weight, norm_gain, queue_keys, new_keys, pointer, positives):
    rows, width = speech.shape
    key_count = queue_keys.shape[0]
    nz = n_queue // GROUP
    vmem = pl.BlockSpec(memory_space=pltpu.VMEM)
    anywhere = pl.BlockSpec(memory_space=pl.ANY)
    dma = pltpu.SemaphoreType.DMA
    bf16, f32 = jnp.bfloat16, jnp.float32
    scratch = [
        pltpu.VMEM((rows, width), bf16),
        pltpu.VMEM(new_keys.shape, bf16),
        pltpu.VMEM((GROUP * key_count, width), bf16),
        pltpu.VMEM((n_mp, width, width // n_mp), bf16),
        pltpu.VMEM((HALVES, nz * rows // HALVES, width), bf16),
        pltpu.VMEM((nz, 8, LANES), jnp.int32),
        pltpu.VMEM((HALVES, nz * rows // HALVES, GROUP * key_count), f32),
        pltpu.VMEM((nz * rows // HALVES, GROUP * key_count), bf16),
        pltpu.VMEM((rows, width), f32),
        pltpu.VMEM((HALVES, width // 256, nz * rows // HALVES, 256), bf16),
        pltpu.VMEM((HALVES, width // 256, nz, rows // HALVES, 256), bf16),
        pltpu.VMEM((HALVES, width // 256, rows // HALVES, 256), bf16),
        pltpu.VMEM((HALVES, nz, nz, 8, LANES), f32),
        pltpu.VMEM((HALVES, nz * rows // HALVES, LANES), f32),
        pltpu.VMEM((HALVES, nz * rows // HALVES, LANES), f32),
        pltpu.VMEM((HALVES, nz * rows // HALVES, LANES), f32),
        pltpu.VMEM((HALVES, nz * rows // HALVES, LANES), jnp.int32),
        dma((4,)),
    ]
    scratch += [dma((n_mp, WEIGHT_CHUNKS))] * 10
    scratch += [dma((1,))] * 2 + [dma((KEY_CHUNKS,))] * 2 + [dma((n_mp, KEY_CHUNKS))] * 2
    scratch += [dma((KEY_CHUNKS,))] * 2 + [dma((n_mp, KEY_CHUNKS))] * 2
    scratch += [dma((HALVES, nz, nz)), dma((HALVES, nz))]
    scratch += [dma((nz,))] * 2 + [dma((HALVES, nz))] * 2
    scratch += [dma((HALVES, width // 256, nz))] * 2 + [dma((HALVES, width // 256))]
    loss, grad, queue_next = pl.pallas_call(
        functools.partial(step_kernel, n_queue, n_mp),
        out_shape=(
            jax.ShapeDtypeStruct((8, LANES), f32),
            jax.ShapeDtypeStruct((rows, width), bf16),
            pltpu.VMEM((key_count, width), bf16),
        ),
        in_specs=[anywhere, anywhere, vmem, anywhere, anywhere, pl.BlockSpec(memory_space=pltpu.SMEM), vmem],
        out_specs=(vmem, vmem, vmem),
        scratch_shapes=scratch,
        compiler_params=pltpu.CompilerParams(
            collective_id=0, has_side_effects=True, vmem_limit_bytes=249 * 256 * 1024
        ),
        name="contrast_step",
    )(speech, weight, norm_gain[None, :], queue_keys, new_keys, pointer, positives[None, :])
    loss, grad, queue_next = pl.pallas_call(
        finish_kernel,
        out_shape=(
            jax.ShapeDtypeStruct((1, rows), f32),
            jax.ShapeDtypeStruct((rows, width), bf16),
            jax.ShapeDtypeStruct((key_count, width), bf16),
        ),
        in_specs=[vmem, anywhere, vmem],
        out_specs=(vmem, anywhere, anywhere),
        scratch_shapes=[
            pltpu.VMEM((rows, width), bf16),
            dma((1,)),
            dma((5,)),
        ],
        compiler_params=pltpu.CompilerParams(vmem_limit_bytes=16 * 1024 * 1024),
        name="hand_out",
    )(loss, grad, queue_next)
    return loss[0], grad, queue_next


def solution(mesh):
    n_queue, n_mp = mesh.shape["queue"], mesh.shape["mp"]
    return jax.shard_map(
        functools.partial(shards, n_queue, n_mp),
        mesh=mesh,
        in_specs=(
            P(("queue", "mp"), None),
            P(None, "mp"),
            P(),
            P("queue", None),
            P(),
            P(),
            P(("queue", "mp")),
        ),
        out_specs=(P(("queue", "mp")), P(("queue", "mp"), None), P("queue", None)),
        check_vma=False,
    )
```

```python
import functools
import math

import jax
import jax.numpy as jnp
from jax import lax
from jax.experimental import pallas as pl
from jax.experimental.pallas import tpu as pltpu
from jax.sharding import PartitionSpec as P

MESH = pl.DeviceIdType.MESH
GROUP = 4
WEIGHT_CHUNKS = 4
KEY_CHUNKS = 6
HALVES = 2
LANES = 128


def column_of(tile, row, count):
    line = jnp.broadcast_to(tile[row : row + 1, :], (LANES, LANES))
    eye = lax.broadcasted_iota(jnp.int32, (LANES, LANES), 0) == lax.broadcasted_iota(
        jnp.int32, (LANES, LANES), 1
    )
    return jnp.sum(jnp.where(eye, line, jnp.zeros_like(line)), axis=1, keepdims=True)[:count]


def row_of(column):
    count = column.shape[0]
    wide = jnp.broadcast_to(column, (count, LANES))
    eye = lax.broadcasted_iota(jnp.int32, (count, LANES), 0) == lax.broadcasted_iota(
        jnp.int32, (count, LANES), 1
    )
    return jnp.sum(jnp.where(eye, wide, jnp.zeros_like(wide)), axis=0, keepdims=True)


def step_kernel(
    n_queue,
    n_mp,
    speech_hbm,
    weight_ref,
    gain_ref,
    keys_ref,
    new_hbm,
    pointer_ref,
    positives_ref,
    loss_ref,
    grad_ref,
    next_ref,
    speech_ref,
    new_ref,
    keys,
    weights_in,
    queries,
    columns,
    scores,
    probs,
    hidden,
    partial,
    arrived,
    relay_in,
    stats,
    wide_peak,
    wide_total,
    wide_positive,
    wide_column,
    local_sem,
    wy_s, wy_r, wx_s, wx_r, wcy_s, wcy_r, wcx_s, wcx_r, wco_s, wco_r,
    kc_s, kc_r, kx_s, kx_r, ky_s, ky_r, kcx_s, kcx_r, kcy_s, kcy_r,
    q_s, q_r, p_s, p_r, st_s, st_r, g_s, g_r, r_r,
):
    rows, width = speech_ref.shape
    key_count = keys_ref.shape[0]
    nz = n_queue // GROUP
    me = lax.axis_index("queue")
    mp = lax.axis_index("mp")
    z = me // GROUP
    slot = me % GROUP
    x = slot // 2
    core = slot % 2
    core_peer = me + 1 - 2 * core
    x_peer = me + 2 - 4 * x
    core_slot = slot + 1 - 2 * core
    x_slot = slot + 2 - 4 * x
    diag_slot = core_slot + 2 - 4 * x

    def z_dev(distance):
        return lax.rem(z + distance, nz) * GROUP + slot

    def mp_dev(distance):
        return lax.rem(mp + distance, n_mp)

    def push(src, dst, send, recv, queue, mp_index):
        return pltpu.make_async_remote_copy(
            src_ref=src, dst_ref=dst, send_sem=send, recv_sem=recv,
            device_id=(queue, mp_index), device_id_type=MESH,
        )

    barrier = pltpu.get_barrier_semaphore()
    peers = [(core_peer, mp), (x_peer, mp)]
    peers += [(me, mp_dev(d)) for d in range(1, n_mp)]
    peers += [(z_dev(d), mp) for d in range(1, nz)]
    for peer in peers:
        pl.semaphore_signal(barrier, inc=1, device_id=peer, device_id_type=MESH)

    def key_rows(which, start, count):
        return keys.at[pl.ds(pl.multiple_of(which * key_count + start, 16), count), :]

    own_keys = pltpu.make_async_copy(keys_ref, key_rows(slot, 0, key_count), local_sem.at[0])
    own_weight = pltpu.make_async_copy(weight_ref, weights_in.at[mp], local_sem.at[1])
    own_speech = pltpu.make_async_copy(speech_hbm, speech_ref, local_sem.at[2])
    own_new = pltpu.make_async_copy(new_hbm, new_ref, local_sem.at[3])
    own_weight.start()
    own_speech.start()
    own_keys.start()
    own_new.start()
    pl.semaphore_wait(barrier, len(peers))

    sends = []
    guarded = []

    def start(copy):
        copy.start()
        sends.append(copy)

    w_count = width // GROUP // WEIGHT_CHUNKS

    def w_push(dist, quarter, j, shard, sems, queue, mp_index, src=None):
        at = pl.ds(pl.multiple_of(quarter * (width // GROUP) + j * w_count, 16), w_count)
        dst = weights_in.at[shard, at, :]
        return push(
            dst if src is None else src.at[at, :], dst,
            sems[0].at[dist, j], sems[1].at[dist, j], queue, mp_index,
        )

    for j in range(WEIGHT_CHUNKS):
        for d in range(1, n_mp):
            start(w_push(d, slot, j, mp, (wy_s, wy_r), me, mp_dev(d), weight_ref))

    part = key_count // n_mp
    k_count = part // KEY_CHUNKS

    def k_start(shard, j):
        return shard * part + j * k_count

    def key_x(j):
        at = k_start(mp, j)
        return push(
            keys_ref.at[pl.ds(pl.multiple_of(at, 16), k_count), :], key_rows(slot, at, k_count),
            kx_s.at[j], kx_r.at[j], x_peer, mp,
        )

    def key_forward(shard, j, send, recv, queue, mp_index, which=x_slot):
        at = key_rows(which, k_start(shard, j), k_count)
        return push(at, at, send, recv, queue, mp_index)

    def key_arrive_x(j):
        key_forward(mp, j, kx_s.at[j], kx_r.at[j], x_peer, mp).wait_recv()
        for d in range(1, n_mp):
            start(key_forward(mp, j, ky_s.at[d, j], ky_r.at[d, j], me, mp_dev(d)))
        start(key_forward(mp, j, kcx_s.at[j], kcx_r.at[j], core_peer, mp))

    def key_arrive_y(j):
        for d in range(1, n_mp):
            shard = mp_dev(n_mp - d)
            key_forward(shard, j, ky_s.at[d, j], ky_r.at[d, j], me, mp).wait_recv()
            start(key_forward(shard, j, kcy_s.at[d, j], kcy_r.at[d, j], core_peer, mp))

    start(key_x(0))

    part_width = width // n_mp

    def encode(shard):
        hidden[:, pl.ds(pl.multiple_of(shard * part_width, LANES), part_width)] = jnp.dot(
            speech_ref[...], weights_in[shard], preferred_element_type=jnp.float32
        )

    own_speech.wait()
    own_weight.wait()
    encode(mp)

    for j in range(WEIGHT_CHUNKS):
        for d in range(1, n_mp):
            shard = mp_dev(n_mp - d)
            w_push(d, slot, j, shard, (wy_s, wy_r), me, mp).wait_recv()
            start(w_push(d, slot, j, shard, (wx_s, wx_r), x_peer, mp))
            start(w_push(d, slot, j, shard, (wcy_s, wcy_r), core_peer, mp))
    for j in range(1, KEY_CHUNKS):
        start(key_x(j))
    for j in range(WEIGHT_CHUNKS):
        for d in range(1, n_mp):
            shard = mp_dev(n_mp - d)
            w_push(d, x_slot, j, shard, (wx_s, wx_r), x_peer, mp).wait_recv()
            start(w_push(d, x_slot, j, shard, (wcx_s, wcx_r), core_peer, mp))
    start(push(keys_ref, key_rows(slot, 0, key_count), kc_s.at[0], kc_r.at[0], core_peer, mp))
    key_arrive_x(0)
    for j in range(WEIGHT_CHUNKS):
        for d in range(1, n_mp):
            shard = mp_dev(n_mp - d)
            w_push(d, core_slot, j, shard, (wcy_s, wcy_r), core_peer, mp).wait_recv()
            w_push(d, diag_slot, j, shard, (wcx_s, wcx_r), core_peer, mp).wait_recv()

    for d in range(1, n_mp):
        encode(mp_dev(n_mp - d))
    encoded = hidden[...]
    inverse_rms = lax.rsqrt(jnp.mean(encoded * encoded, axis=1, keepdims=True) + 1e-06)
    part_rows = rows // HALVES
    normed = (encoded * inverse_rms * gain_ref[...]).astype(jnp.bfloat16)
    for h in range(HALVES):
        queries[h, pl.ds(pl.multiple_of(z * part_rows, 16), part_rows), :] = normed[
            h * part_rows : (h + 1) * part_rows
        ]
    columns[z, 0:1, 0:rows] = positives_ref[...]

    def z_rows(index):
        return pl.ds(pl.multiple_of(index * part_rows, 16), part_rows)


    def guarded_start(condition, make):
        @pl.when(condition)
        def _():
            make().start()

        guarded.append((condition, make))

    relayed = nz > 2

    def query_push(h, owner, target):
        at = queries.at[h, z_rows(owner), :]
        return push(
            at, at, q_s.at[h, owner, target], q_r.at[h, owner], target * GROUP + slot, mp
        )

    def column_push(d, owner, target):
        at = columns.at[owner]
        return push(at, at, p_s.at[d], p_r.at[d], target, mp)

    def between_ends(source, target):
        if not relayed:
            return source != source
        low = (source == 0) & (target == nz - 1)
        return low | ((source == nz - 1) & (target == 0))

    for h in range(HALVES):
        for distance in range(nz - 1, 0, -1):
            for target in (z + distance, z - distance):
                there = (target >= 0) & (target < nz)
                guarded_start(
                    there & jnp.logical_not(between_ends(z, target)),
                    functools.partial(query_push, h, z, target),
                )
    for d in range(1, nz):
        start(column_push(d, z, z_dev(d)))

    def query_relay(h):
        for owner, via, target in ((0, nz - 2, nz - 1), (nz - 1, 1, 0)):

            @pl.when(z == via)
            def _():
                query_push(h, owner, via).wait_recv()

            guarded_start(z == via, functools.partial(query_push, h, owner, target))

    def take_rows(step):
        block = key_count // 3
        at = pl.ds(step * block, block)
        length = key_count * n_queue
        ids = me * key_count + step * block + lax.broadcasted_iota(jnp.int32, (block, 1), 0)
        offsets = ids - pointer_ref[0]
        offsets = jnp.where(offsets < 0, offsets + length, offsets)
        count = new_ref.shape[0]
        chosen = lax.broadcasted_iota(jnp.int32, (block, count), 1) == offsets
        taken = jnp.dot(
            jnp.where(chosen, 1.0, 0.0).astype(jnp.bfloat16), new_ref[...],
            preferred_element_type=jnp.float32,
        )
        held = keys[pl.ds(pl.multiple_of(slot * key_count + step * block, 16), block), :]
        next_ref[at, :] = jnp.where(offsets < count, taken, held.astype(jnp.float32)).astype(
            jnp.bfloat16
        )

    own_keys.wait()
    for j in range(1, KEY_CHUNKS):
        key_arrive_x(j)
        if j == 1:
            own_new.wait()
        if j <= 3:
            take_rows(j - 1)
        if j > 1:
            key_arrive_y(j - 2)
        if j >= KEY_CHUNKS - HALVES and relayed:
            query_relay(j - KEY_CHUNKS + HALVES)
    for j in range(KEY_CHUNKS - 2, KEY_CHUNKS):
        key_arrive_y(j)
    push(
        keys_ref, key_rows(core_slot, 0, key_count), kc_s.at[0], kc_r.at[0], core_peer, mp
    ).wait_recv()
    def diagonal_arrive():
        for j in range(KEY_CHUNKS):
            key_forward(mp, j, kcx_s.at[j], kcx_r.at[j], core_peer, mp, diag_slot).wait_recv()
            for d in range(1, n_mp):
                shard = mp_dev(n_mp - d)
                key_forward(
                    shard, j, kcy_s.at[d, j], kcy_r.at[d, j], core_peer, mp, diag_slot
                ).wait_recv()

    def queries_arrive(h):
        for owner in range(nz):
            waiting = z != owner
            if relayed and owner in (0, nz - 1):
                waiting = waiting & (z != (nz - 2 if owner == 0 else 1))

            @pl.when(waiting)
            def _():
                query_push(h, owner, z).wait_recv()

    for d in range(1, nz):
        column_push(d, lax.rem(z + nz - d, nz), me).wait_recv()

    factor = 2.0 / math.sqrt(width)
    total_rows = nz * part_rows
    total_keys = GROUP * key_count
    block = 256
    n_steps = key_count // block
    for i in range(nz):
        tile = column_of(columns[i], 0, rows) - z * total_keys
        for h in range(HALVES):
            wide_column[h, i * part_rows : (i + 1) * part_rows, :] = jnp.broadcast_to(
                tile[h * part_rows : (h + 1) * part_rows], (part_rows, LANES)
            )
    wide_peak[...] = jnp.full(wide_peak.shape, -1e30, jnp.float32)
    wide_total[...] = jnp.zeros(wide_total.shape, jnp.float32)
    wide_positive[...] = jnp.zeros(wide_positive.shape, jnp.float32)

    def is_positive(h, start):
        ids = start + lax.broadcasted_iota(jnp.int32, (total_rows, LANES), 1)
        return ids == wide_column[h]

    def score_keys(h, which):
        @pl.loop(0, n_steps)
        def _(step):
            first = pl.multiple_of(which * key_count + step * block, block)
            at = pl.ds(first, block)
            product = (
                lax.dot_general(
                    queries[h], keys[at, :], (((1,), (1,)), ((), ())),
                    preferred_element_type=jnp.float32,
                )
                * factor
            )
            scores[h, :, at] = product
            peak = wide_peak[h]
            positive = wide_positive[h]
            for half in range(block // LANES):
                piece = product[:, half * LANES : (half + 1) * LANES]
                peak = jnp.maximum(peak, piece)
                positive = positive + jnp.where(is_positive(h, first + half * LANES), piece, 0.0)
            wide_peak[h] = peak
            wide_positive[h] = positive

    def stats_push(h, d, owner, target):
        at = stats.at[h, owner]
        return push(at, at, st_s.at[h, d], st_r.at[h, d], target, mp)

    def local_stats(h):
        peak = jnp.max(wide_peak[h], axis=1, keepdims=True)
        wide_peak[h] = jnp.broadcast_to(peak, (total_rows, LANES))

        @pl.loop(0, total_keys // block)
        def _(step):
            total = wide_total[h]
            for half in range(block // LANES):
                at = pl.ds(pl.multiple_of(step * block + half * LANES, LANES), LANES)
                power = jnp.exp(scores[h, :, at] - wide_peak[h])
                scores[h, :, at] = power
                total = total + power
            wide_total[h] = total

        total = jnp.sum(wide_total[h], axis=1, keepdims=True)
        positive = jnp.sum(wide_positive[h], axis=1, keepdims=True)
        for i in range(nz):
            at = slice(i * part_rows, (i + 1) * part_rows)
            stats[h, z, i, 0:1, :] = row_of(peak[at])
            stats[h, z, i, 1:2, :] = row_of(total[at])
            stats[h, z, i, 2:3, :] = row_of(positive[at])
        for d in range(1, nz):
            start(stats_push(h, d, z, z_dev(d)))
        return peak

    def weights_of(h, peak):
        for d in range(1, nz):
            stats_push(h, d, lax.rem(z + nz - d, nz), me).wait_recv()
        top = stats[h, 0, :, 0, :]
        for i in range(1, nz):
            top = jnp.maximum(top, stats[h, i, :, 0, :])
        whole = jnp.zeros_like(top)
        found = jnp.zeros_like(top)
        for i in range(nz):
            whole = whole + stats[h, i, :, 1, :] * jnp.exp(stats[h, i, :, 0, :] - top)
            found = found + stats[h, i, :, 2, :]
        log_rows = top + jnp.log(jnp.maximum(whole, 1e-30))
        losses = log_rows - found
        loss_line = jnp.zeros((1, LANES), jnp.float32)
        for i in range(nz):
            loss_line = loss_line + jnp.where(z == i, losses[i : i + 1, :], 0.0)
        loss_ref[h : h + 1, :] = loss_line
        log_total = jnp.concatenate(
            [column_of(log_rows[i : i + 1, :], 0, part_rows) for i in range(nz)], axis=0
        )
        wide_total[h] = jnp.broadcast_to(jnp.exp(peak - log_total), (total_rows, LANES))

        @pl.loop(0, total_keys // block)
        def _(step):
            for half in range(block // LANES):
                start_at = pl.multiple_of(step * block + half * LANES, LANES)
                at = pl.ds(start_at, LANES)
                probs[:, at] = (
                    scores[h, :, at] * wide_total[h]
                    - jnp.where(is_positive(h, start_at), 1.0, 0.0)
                ).astype(jnp.bfloat16)

    for h in range(HALVES):
        queries_arrive(h)
        score_keys(h, slot)
        score_keys(h, core_slot)
    diagonal_arrive()
    peaks = []
    for h in range(HALVES):
        score_keys(h, x_slot)
        score_keys(h, diag_slot)
        peaks.append(local_stats(h))

    n_blocks = width // block

    def grad_push(h, c, owner, source, target):
        return push(
            partial.at[h, c, z_rows(owner), :], arrived.at[h, c, source],
            g_s.at[h, c, owner], g_r.at[h, c, source], target * GROUP + slot, mp,
        )

    def grad_relay_push(h, c, owner, target):
        return push(
            partial.at[h, c, z_rows(owner), :], relay_in.at[h, c],
            g_s.at[h, c, owner], r_r.at[h, c], target * GROUP + slot, mp,
        )

    def grad_relay(h, c):
        for source, via, owner in ((0, 1, nz - 1), (nz - 1, nz - 2, 0)):

            @pl.when(z == via)
            def _():
                grad_relay_push(h, c, owner, via).wait_recv()
                at = slice(owner * part_rows, (owner + 1) * part_rows)
                partial[h, c, at, :] = (
                    partial[h, c, at, :].astype(jnp.float32) + relay_in[h, c].astype(jnp.float32)
                ).astype(jnp.bfloat16)

            guarded_start(z == via, functools.partial(grad_push, h, c, owner, via, owner))

    waiting_relays = []
    for h in range(HALVES):
        weights_of(h, peaks[h])
        for c in range(n_blocks):
            partial[h, c] = jnp.dot(
                probs[...], keys[:, c * block : (c + 1) * block],
                preferred_element_type=jnp.float32,
            ).astype(jnp.bfloat16)
            if relayed:
                guarded_start(z == 0, functools.partial(grad_relay_push, h, c, nz - 1, 1))
                guarded_start(z == nz - 1, functools.partial(grad_relay_push, h, c, 0, nz - 2))
                waiting_relays.append((h, c))
            for distance in range(nz - 1, 0, -1):
                for owner in (z + distance, z - distance):
                    there = (owner >= 0) & (owner < nz) & jnp.logical_not(between_ends(z, owner))
                    if relayed:
                        there = there & jnp.logical_not((z == 1) & (owner == nz - 1))
                        there = there & jnp.logical_not((z == nz - 2) & (owner == 0))
                    guarded_start(there, functools.partial(grad_push, h, c, owner, z, owner))
            if len(waiting_relays) > 2:
                grad_relay(*waiting_relays.pop(0))
    for late in waiting_relays:
        grad_relay(*late)

    scaled = []
    inner = jnp.zeros((rows, 1), jnp.float32)
    for c in range(n_blocks):
        sums = []
        for h in range(HALVES):
            for source in range(nz):
                absent = (z == source) | between_ends(z, jnp.int32(source))

                @pl.when(jnp.logical_not(absent))
                def _():
                    grad_push(h, c, z, source, z).wait_recv()

                @pl.when(absent)
                def _():
                    arrived[h, c, source] = jnp.zeros((part_rows, block), jnp.bfloat16)

            summed = partial[h, c, z_rows(z), :].astype(jnp.float32)
            for source in range(nz):
                summed = summed + arrived[h, c, source].astype(jnp.float32)
            sums.append(summed)
        at = slice(c * block, (c + 1) * block)
        block_scaled = gain_ref[:, at] * (jnp.concatenate(sums, axis=0) * (16.0 * factor))
        scaled.append(block_scaled)
        inner = inner + jnp.sum(block_scaled * hidden[:, at], axis=1, keepdims=True)
    inner = inverse_rms * inverse_rms * inverse_rms * inner / width
    hidden_grad = jnp.concatenate(
        [
            (inverse_rms * scaled[c] - hidden[:, c * block : (c + 1) * block] * inner).astype(
                jnp.bfloat16
            )
            for c in range(n_blocks)
        ],
        axis=1,
    )
    result = jnp.zeros((rows, width), jnp.float32)
    for m in range(n_mp):
        result = result + lax.dot_general(
            hidden_grad[:, m * part_width : (m + 1) * part_width], weights_in[m],
            (((1,), (1,)), ((), ())), preferred_element_type=jnp.float32,
        )
    grad_ref[...] = result.astype(jnp.bfloat16)
    for copy in sends:
        copy.wait_send()
    for condition, make in guarded:

        @pl.when(condition)
        def _(make=make):
            make().wait_send()


def finish_kernel(
    loss_in, grad_in, next_in, loss_ref, grad_ref, next_ref, sem_out
):
    count = next_in.shape[0] // 4
    stores = [pltpu.make_async_copy(grad_in, grad_ref, sem_out.at[4])]
    stores[0].start()
    for i in range(4):
        at = pl.ds(i * count, count)
        stores.append(pltpu.make_async_copy(next_in.at[at], next_ref.at[at], sem_out.at[i]))
        stores[-1].start()
    count = loss_ref.shape[1] // HALVES
    for h in range(HALVES):
        loss_ref[:, h * count : (h + 1) * count] = loss_in[h : h + 1, 0:count]
    for store in stores:
        store.wait()


def shards(n_queue, n_mp, speech, weight, norm_gain, queue_keys, new_keys, pointer, positives):
    rows, width = speech.shape
    key_count = queue_keys.shape[0]
    nz = n_queue // GROUP
    vmem = pl.BlockSpec(memory_space=pltpu.VMEM)
    anywhere = pl.BlockSpec(memory_space=pl.ANY)
    dma = pltpu.SemaphoreType.DMA
    bf16, f32 = jnp.bfloat16, jnp.float32
    scratch = [
        pltpu.VMEM((rows, width), bf16),
        pltpu.VMEM(new_keys.shape, bf16),
        pltpu.VMEM((GROUP * key_count, width), bf16),
        pltpu.VMEM((n_mp, width, width // n_mp), bf16),
        pltpu.VMEM((HALVES, nz * rows // HALVES, width), bf16),
        pltpu.VMEM((nz, 8, LANES), jnp.int32),
        pltpu.VMEM((HALVES, nz * rows // HALVES, GROUP * key_count), f32),
        pltpu.VMEM((nz * rows // HALVES, GROUP * key_count), bf16),
        pltpu.VMEM((rows, width), f32),
        pltpu.VMEM((HALVES, width // 256, nz * rows // HALVES, 256), bf16),
        pltpu.VMEM((HALVES, width // 256, nz, rows // HALVES, 256), bf16),
        pltpu.VMEM((HALVES, width // 256, rows // HALVES, 256), bf16),
        pltpu.VMEM((HALVES, nz, nz, 8, LANES), f32),
        pltpu.VMEM((HALVES, nz * rows // HALVES, LANES), f32),
        pltpu.VMEM((HALVES, nz * rows // HALVES, LANES), f32),
        pltpu.VMEM((HALVES, nz * rows // HALVES, LANES), f32),
        pltpu.VMEM((HALVES, nz * rows // HALVES, LANES), jnp.int32),
        dma((4,)),
    ]
    scratch += [dma((n_mp, WEIGHT_CHUNKS))] * 10
    scratch += [dma((1,))] * 2 + [dma((KEY_CHUNKS,))] * 2 + [dma((n_mp, KEY_CHUNKS))] * 2
    scratch += [dma((KEY_CHUNKS,))] * 2 + [dma((n_mp, KEY_CHUNKS))] * 2
    scratch += [dma((HALVES, nz, nz)), dma((HALVES, nz))]
    scratch += [dma((nz,))] * 2 + [dma((HALVES, nz))] * 2
    scratch += [dma((HALVES, width // 256, nz))] * 2 + [dma((HALVES, width // 256))]
    loss, grad, queue_next = pl.pallas_call(
        functools.partial(step_kernel, n_queue, n_mp),
        out_shape=(
            pltpu.VMEM((8, LANES), f32),
            pltpu.VMEM((rows, width), bf16),
            pltpu.VMEM((key_count, width), bf16),
        ),
        in_specs=[anywhere, anywhere, vmem, anywhere, anywhere, pl.BlockSpec(memory_space=pltpu.SMEM), vmem],
        out_specs=(vmem, vmem, vmem),
        scratch_shapes=scratch,
        compiler_params=pltpu.CompilerParams(
            collective_id=0, has_side_effects=True, vmem_limit_bytes=248 * 256 * 1024
        ),
        name="contrast_step",
    )(speech, weight, norm_gain[None, :], queue_keys, new_keys, pointer, positives[None, :])
    loss, grad, queue_next = pl.pallas_call(
        finish_kernel,
        out_shape=(
            jax.ShapeDtypeStruct((1, rows), f32),
            jax.ShapeDtypeStruct((rows, width), bf16),
            jax.ShapeDtypeStruct((key_count, width), bf16),
        ),
        in_specs=[vmem, vmem, vmem],
        out_specs=(vmem, anywhere, anywhere),
        scratch_shapes=[
            dma((5,)),
        ],
        compiler_params=pltpu.CompilerParams(vmem_limit_bytes=16 * 1024 * 1024),
        name="hand_out",
    )(loss, grad, queue_next)
    return loss[0], grad, queue_next


def solution(mesh):
    n_queue, n_mp = mesh.shape["queue"], mesh.shape["mp"]
    return jax.shard_map(
        functools.partial(shards, n_queue, n_mp),
        mesh=mesh,
        in_specs=(
            P(("queue", "mp"), None),
            P(None, "mp"),
            P(),
            P("queue", None),
            P(),
            P(),
            P(("queue", "mp")),
        ),
        out_specs=(P(("queue", "mp")), P(("queue", "mp"), None), P("queue", None)),
        check_vma=False,
    )
```

```python
import functools
import math

import jax
import jax.numpy as jnp
from jax import lax
from jax.experimental import pallas as pl
from jax.experimental.pallas import tpu as pltpu
from jax.sharding import PartitionSpec as P

MESH = pl.DeviceIdType.MESH
GROUP = 4
WEIGHT_CHUNKS = 4
HALVES = 2
LANES = 128


def key_chunks(part):
    return 12 if part % (12 * 16) == 0 else 6


def column_of(tile, row, count):
    line = jnp.broadcast_to(tile[row : row + 1, :], (LANES, LANES))
    eye = lax.broadcasted_iota(jnp.int32, (LANES, LANES), 0) == lax.broadcasted_iota(
        jnp.int32, (LANES, LANES), 1
    )
    return jnp.sum(jnp.where(eye, line, jnp.zeros_like(line)), axis=1, keepdims=True)[:count]


def row_of(column):
    count = column.shape[0]
    wide = jnp.broadcast_to(column, (count, LANES))
    eye = lax.broadcasted_iota(jnp.int32, (count, LANES), 0) == lax.broadcasted_iota(
        jnp.int32, (count, LANES), 1
    )
    return jnp.sum(jnp.where(eye, wide, jnp.zeros_like(wide)), axis=0, keepdims=True)


def step_kernel(
    n_queue,
    n_mp,
    speech_hbm,
    weight_ref,
    gain_ref,
    keys_ref,
    new_hbm,
    pointer_ref,
    positives_ref,
    loss_ref,
    grad_ref,
    next_ref,
    speech_ref,
    new_ref,
    keys,
    weights_in,
    queries,
    columns,
    scores,
    probs,
    hidden,
    partial,
    arrived,
    relay_in,
    stats,
    wide_peak,
    wide_total,
    wide_positive,
    wide_column,
    local_sem,
    wy_s, wy_r, wx_s, wx_r, wcy_s, wcy_r, wcx_s, wcx_r, wco_s, wco_r,
    kc_s, kc_r, kx_s, kx_r, ky_s, ky_r, kcx_s, kcx_r, kcy_s, kcy_r,
    q_s, q_r, p_s, p_r, st_s, st_r, g_s, g_r, r_r,
):
    rows, width = speech_ref.shape
    key_count = keys_ref.shape[0]
    nz = n_queue // GROUP
    me = lax.axis_index("queue")
    mp = lax.axis_index("mp")
    z = me // GROUP
    slot = me % GROUP
    x = slot // 2
    core = slot % 2
    core_peer = me + 1 - 2 * core
    x_peer = me + 2 - 4 * x
    core_slot = slot + 1 - 2 * core
    x_slot = slot + 2 - 4 * x
    diag_slot = core_slot + 2 - 4 * x

    def z_dev(distance):
        return lax.rem(z + distance, nz) * GROUP + slot

    def mp_dev(distance):
        return lax.rem(mp + distance, n_mp)

    def push(src, dst, send, recv, queue, mp_index):
        return pltpu.make_async_remote_copy(
            src_ref=src, dst_ref=dst, send_sem=send, recv_sem=recv,
            device_id=(queue, mp_index), device_id_type=MESH,
        )

    barrier = pltpu.get_barrier_semaphore()
    peers = [(core_peer, mp), (x_peer, mp)]
    peers += [(me, mp_dev(d)) for d in range(1, n_mp)]
    peers += [(z_dev(d), mp) for d in range(1, nz)]
    for peer in peers:
        pl.semaphore_signal(barrier, inc=1, device_id=peer, device_id_type=MESH)

    def key_rows(which, start, count):
        return keys.at[pl.ds(pl.multiple_of(which * key_count + start, 16), count), :]

    own_keys = pltpu.make_async_copy(keys_ref, key_rows(slot, 0, key_count), local_sem.at[0])
    own_weight = pltpu.make_async_copy(weight_ref, weights_in.at[mp], local_sem.at[1])
    own_speech = pltpu.make_async_copy(speech_hbm, speech_ref, local_sem.at[2])
    own_new = pltpu.make_async_copy(new_hbm, new_ref, local_sem.at[3])
    own_weight.start()
    own_speech.start()
    own_keys.start()
    own_new.start()
    pl.semaphore_wait(barrier, len(peers))

    sends = []
    guarded = []

    def start(copy):
        copy.start()
        sends.append(copy)

    w_count = width // GROUP // WEIGHT_CHUNKS

    def w_push(dist, quarter, j, shard, sems, queue, mp_index, src=None):
        at = pl.ds(pl.multiple_of(quarter * (width // GROUP) + j * w_count, 16), w_count)
        dst = weights_in.at[shard, at, :]
        return push(
            dst if src is None else src.at[at, :], dst,
            sems[0].at[dist, j], sems[1].at[dist, j], queue, mp_index,
        )

    for j in range(WEIGHT_CHUNKS):
        for d in range(1, n_mp):
            start(w_push(d, slot, j, mp, (wy_s, wy_r), me, mp_dev(d), weight_ref))

    part = key_count // n_mp
    n_chunks = key_chunks(part)
    k_count = part // n_chunks

    def k_start(shard, j):
        return shard * part + j * k_count

    def key_x(j):
        at = k_start(mp, j)
        return push(
            keys_ref.at[pl.ds(pl.multiple_of(at, 16), k_count), :], key_rows(slot, at, k_count),
            kx_s.at[j], kx_r.at[j], x_peer, mp,
        )

    def key_forward(shard, j, send, recv, queue, mp_index, which=x_slot):
        at = key_rows(which, k_start(shard, j), k_count)
        return push(at, at, send, recv, queue, mp_index)

    def key_arrive_x(j):
        key_forward(mp, j, kx_s.at[j], kx_r.at[j], x_peer, mp).wait_recv()
        for d in range(1, n_mp):
            start(key_forward(mp, j, ky_s.at[d, j], ky_r.at[d, j], me, mp_dev(d)))
        start(key_forward(mp, j, kcx_s.at[j], kcx_r.at[j], core_peer, mp))

    def key_arrive_y(j):
        for d in range(1, n_mp):
            shard = mp_dev(n_mp - d)
            key_forward(shard, j, ky_s.at[d, j], ky_r.at[d, j], me, mp).wait_recv()
            start(key_forward(shard, j, kcy_s.at[d, j], kcy_r.at[d, j], core_peer, mp))

    start(key_x(0))

    part_width = width // n_mp

    def encode(shard):
        hidden[:, pl.ds(pl.multiple_of(shard * part_width, LANES), part_width)] = jnp.dot(
            speech_ref[...], weights_in[shard], preferred_element_type=jnp.float32
        )

    own_speech.wait()
    own_weight.wait()
    encode(mp)

    for j in range(WEIGHT_CHUNKS):
        for d in range(1, n_mp):
            shard = mp_dev(n_mp - d)
            w_push(d, slot, j, shard, (wy_s, wy_r), me, mp).wait_recv()
            start(w_push(d, slot, j, shard, (wx_s, wx_r), x_peer, mp))
            start(w_push(d, slot, j, shard, (wcy_s, wcy_r), core_peer, mp))
    for j in range(1, n_chunks):
        start(key_x(j))
    for j in range(WEIGHT_CHUNKS):
        for d in range(1, n_mp):
            shard = mp_dev(n_mp - d)
            w_push(d, x_slot, j, shard, (wx_s, wx_r), x_peer, mp).wait_recv()
            start(w_push(d, x_slot, j, shard, (wcx_s, wcx_r), core_peer, mp))
    start(push(keys_ref, key_rows(slot, 0, key_count), kc_s.at[0], kc_r.at[0], core_peer, mp))
    key_arrive_x(0)
    for j in range(WEIGHT_CHUNKS):
        for d in range(1, n_mp):
            shard = mp_dev(n_mp - d)
            w_push(d, core_slot, j, shard, (wcy_s, wcy_r), core_peer, mp).wait_recv()
            w_push(d, diag_slot, j, shard, (wcx_s, wcx_r), core_peer, mp).wait_recv()

    for d in range(1, n_mp):
        encode(mp_dev(n_mp - d))
    encoded = hidden[...]
    inverse_rms = lax.rsqrt(jnp.mean(encoded * encoded, axis=1, keepdims=True) + 1e-06)
    part_rows = rows // HALVES
    normed = (encoded * inverse_rms * gain_ref[...]).astype(jnp.bfloat16)
    for h in range(HALVES):
        queries[h, pl.ds(pl.multiple_of(z * part_rows, 16), part_rows), :] = normed[
            h * part_rows : (h + 1) * part_rows
        ]
    columns[z, 0:1, 0:rows] = positives_ref[...]

    def z_rows(index):
        return pl.ds(pl.multiple_of(index * part_rows, 16), part_rows)


    def guarded_start(condition, make):
        @pl.when(condition)
        def _():
            make().start()

        guarded.append((condition, make))

    relayed = nz > 2

    def query_push(h, owner, target):
        at = queries.at[h, z_rows(owner), :]
        return push(
            at, at, q_s.at[h, owner, target], q_r.at[h, owner], target * GROUP + slot, mp
        )

    def column_push(d, owner, target):
        at = columns.at[owner]
        return push(at, at, p_s.at[d], p_r.at[d], target, mp)

    def between_ends(source, target):
        if not relayed:
            return source != source
        low = (source == 0) & (target == nz - 1)
        return low | ((source == nz - 1) & (target == 0))

    for h in range(HALVES):
        for distance in range(nz - 1, 0, -1):
            for target in (z + distance, z - distance):
                there = (target >= 0) & (target < nz)
                guarded_start(
                    there & jnp.logical_not(between_ends(z, target)),
                    functools.partial(query_push, h, z, target),
                )
    for d in range(1, nz):
        start(column_push(d, z, z_dev(d)))

    def query_relay(h):
        for owner, via, target in ((0, nz - 2, nz - 1), (nz - 1, 1, 0)):

            @pl.when(z == via)
            def _():
                query_push(h, owner, via).wait_recv()

            guarded_start(z == via, functools.partial(query_push, h, owner, target))

    def take_rows(step):
        block = key_count // 3
        at = pl.ds(step * block, block)
        length = key_count * n_queue
        ids = me * key_count + step * block + lax.broadcasted_iota(jnp.int32, (block, 1), 0)
        offsets = ids - pointer_ref[0]
        offsets = jnp.where(offsets < 0, offsets + length, offsets)
        count = new_ref.shape[0]
        chosen = lax.broadcasted_iota(jnp.int32, (block, count), 1) == offsets
        taken = jnp.dot(
            jnp.where(chosen, 1.0, 0.0).astype(jnp.bfloat16), new_ref[...],
            preferred_element_type=jnp.float32,
        )
        held = keys[pl.ds(pl.multiple_of(slot * key_count + step * block, 16), block), :]
        next_ref[at, :] = jnp.where(offsets < count, taken, held.astype(jnp.float32)).astype(
            jnp.bfloat16
        )

    own_keys.wait()
    for j in range(1, n_chunks):
        key_arrive_x(j)
        if j == 1:
            own_new.wait()
        if j <= 3:
            take_rows(j - 1)
        if j > 1:
            key_arrive_y(j - 2)
        for h in range(HALVES):
            if relayed and j == (4 + h) * n_chunks // 6:
                query_relay(h)
    push(
        keys_ref, key_rows(core_slot, 0, key_count), kc_s.at[0], kc_r.at[0], core_peer, mp
    ).wait_recv()
    def diagonal_arrive():
        for j in range(n_chunks):
            key_forward(mp, j, kcx_s.at[j], kcx_r.at[j], core_peer, mp, diag_slot).wait_recv()
            for d in range(1, n_mp):
                shard = mp_dev(n_mp - d)
                key_forward(
                    shard, j, kcy_s.at[d, j], kcy_r.at[d, j], core_peer, mp, diag_slot
                ).wait_recv()

    def queries_arrive(h):
        for owner in range(nz):
            waiting = z != owner
            if relayed and owner in (0, nz - 1):
                waiting = waiting & (z != (nz - 2 if owner == 0 else 1))

            @pl.when(waiting)
            def _():
                query_push(h, owner, z).wait_recv()

    for d in range(1, nz):
        column_push(d, lax.rem(z + nz - d, nz), me).wait_recv()

    factor = 2.0 / math.sqrt(width)
    total_rows = nz * part_rows
    total_keys = GROUP * key_count
    block = 256
    n_steps = key_count // block
    for i in range(nz):
        tile = column_of(columns[i], 0, rows) - z * total_keys
        for h in range(HALVES):
            wide_column[h, i * part_rows : (i + 1) * part_rows, :] = jnp.broadcast_to(
                tile[h * part_rows : (h + 1) * part_rows], (part_rows, LANES)
            )
    wide_peak[...] = jnp.full(wide_peak.shape, -1e30, jnp.float32)
    wide_total[...] = jnp.zeros(wide_total.shape, jnp.float32)
    wide_positive[...] = jnp.zeros(wide_positive.shape, jnp.float32)

    def is_positive(h, start):
        ids = start + lax.broadcasted_iota(jnp.int32, (total_rows, LANES), 1)
        return ids == wide_column[h]

    def score_keys(h, which):
        @pl.loop(0, n_steps)
        def _(step):
            first = pl.multiple_of(which * key_count + step * block, block)
            at = pl.ds(first, block)
            product = (
                lax.dot_general(
                    queries[h], keys[at, :], (((1,), (1,)), ((), ())),
                    preferred_element_type=jnp.float32,
                )
                * factor
            )
            scores[h, :, at] = product
            peak = wide_peak[h]
            positive = wide_positive[h]
            for half in range(block // LANES):
                piece = product[:, half * LANES : (half + 1) * LANES]
                peak = jnp.maximum(peak, piece)
                positive = positive + jnp.where(is_positive(h, first + half * LANES), piece, 0.0)
            wide_peak[h] = peak
            wide_positive[h] = positive

    def stats_push(h, d, owner, target):
        at = stats.at[h, owner]
        return push(at, at, st_s.at[h, d], st_r.at[h, d], target, mp)

    def local_stats(h):
        peak = jnp.max(wide_peak[h], axis=1, keepdims=True)
        wide_peak[h] = jnp.broadcast_to(peak, (total_rows, LANES))

        @pl.loop(0, total_keys // block)
        def _(step):
            total = wide_total[h]
            for half in range(block // LANES):
                at = pl.ds(pl.multiple_of(step * block + half * LANES, LANES), LANES)
                power = jnp.exp(scores[h, :, at] - wide_peak[h])
                scores[h, :, at] = power
                total = total + power
            wide_total[h] = total

        total = jnp.sum(wide_total[h], axis=1, keepdims=True)
        positive = jnp.sum(wide_positive[h], axis=1, keepdims=True)
        for i in range(nz):
            at = slice(i * part_rows, (i + 1) * part_rows)
            stats[h, z, i, 0:1, :] = row_of(peak[at])
            stats[h, z, i, 1:2, :] = row_of(total[at])
            stats[h, z, i, 2:3, :] = row_of(positive[at])
        for d in range(1, nz):
            start(stats_push(h, d, z, z_dev(d)))
        return peak

    def weights_of(h, peak):
        for d in range(1, nz):
            stats_push(h, d, lax.rem(z + nz - d, nz), me).wait_recv()
        top = stats[h, 0, :, 0, :]
        for i in range(1, nz):
            top = jnp.maximum(top, stats[h, i, :, 0, :])
        whole = jnp.zeros_like(top)
        found = jnp.zeros_like(top)
        for i in range(nz):
            whole = whole + stats[h, i, :, 1, :] * jnp.exp(stats[h, i, :, 0, :] - top)
            found = found + stats[h, i, :, 2, :]
        log_rows = top + jnp.log(jnp.maximum(whole, 1e-30))
        losses = log_rows - found
        loss_line = jnp.zeros((1, LANES), jnp.float32)
        for i in range(nz):
            loss_line = loss_line + jnp.where(z == i, losses[i : i + 1, :], 0.0)
        loss_ref[h : h + 1, :] = loss_line
        log_total = jnp.concatenate(
            [column_of(log_rows[i : i + 1, :], 0, part_rows) for i in range(nz)], axis=0
        )
        wide_total[h] = jnp.broadcast_to(jnp.exp(peak - log_total), (total_rows, LANES))

        @pl.loop(0, total_keys // block)
        def _(step):
            for half in range(block // LANES):
                start_at = pl.multiple_of(step * block + half * LANES, LANES)
                at = pl.ds(start_at, LANES)
                probs[:, at] = (
                    scores[h, :, at] * wide_total[h]
                    - jnp.where(is_positive(h, start_at), 1.0, 0.0)
                ).astype(jnp.bfloat16)

    for h in range(HALVES):
        queries_arrive(h)
        score_keys(h, slot)
        if h == 0:
            key_arrive_y(n_chunks - 2)
        score_keys(h, core_slot)
        if h == 0:
            key_arrive_y(n_chunks - 1)
    diagonal_arrive()
    peaks = []
    for h in range(HALVES):
        score_keys(h, x_slot)
        score_keys(h, diag_slot)
        peaks.append(local_stats(h))

    n_blocks = width // block

    def grad_push(h, c, owner, source, target):
        return push(
            partial.at[h, c, z_rows(owner), :], arrived.at[h, c, source],
            g_s.at[h, c, owner], g_r.at[h, c, source], target * GROUP + slot, mp,
        )

    def grad_relay_push(h, c, owner, target):
        return push(
            partial.at[h, c, z_rows(owner), :], relay_in.at[h, c],
            g_s.at[h, c, owner], r_r.at[h, c], target * GROUP + slot, mp,
        )

    def grad_relay(h, c):
        for source, via, owner in ((0, 1, nz - 1), (nz - 1, nz - 2, 0)):

            @pl.when(z == via)
            def _():
                grad_relay_push(h, c, owner, via).wait_recv()
                at = slice(owner * part_rows, (owner + 1) * part_rows)
                partial[h, c, at, :] = (
                    partial[h, c, at, :].astype(jnp.float32) + relay_in[h, c].astype(jnp.float32)
                ).astype(jnp.bfloat16)

            guarded_start(z == via, functools.partial(grad_push, h, c, owner, via, owner))

    waiting_relays = []
    for h in range(HALVES):
        weights_of(h, peaks[h])
        for c in range(n_blocks):
            partial[h, c] = jnp.dot(
                probs[...], keys[:, c * block : (c + 1) * block],
                preferred_element_type=jnp.float32,
            ).astype(jnp.bfloat16)
            if relayed:
                guarded_start(z == 0, functools.partial(grad_relay_push, h, c, nz - 1, 1))
                guarded_start(z == nz - 1, functools.partial(grad_relay_push, h, c, 0, nz - 2))
                waiting_relays.append((h, c))
            for distance in range(nz - 1, 0, -1):
                for owner in (z + distance, z - distance):
                    there = (owner >= 0) & (owner < nz) & jnp.logical_not(between_ends(z, owner))
                    if relayed:
                        there = there & jnp.logical_not((z == 1) & (owner == nz - 1))
                        there = there & jnp.logical_not((z == nz - 2) & (owner == 0))
                    guarded_start(there, functools.partial(grad_push, h, c, owner, z, owner))
            if len(waiting_relays) > 2:
                grad_relay(*waiting_relays.pop(0))
    for late in waiting_relays:
        grad_relay(*late)

    scaled = []
    inner = jnp.zeros((rows, 1), jnp.float32)
    for c in range(n_blocks):
        sums = []
        for h in range(HALVES):
            for source in range(nz):
                absent = (z == source) | between_ends(z, jnp.int32(source))

                @pl.when(jnp.logical_not(absent))
                def _():
                    grad_push(h, c, z, source, z).wait_recv()

                @pl.when(absent)
                def _():
                    arrived[h, c, source] = jnp.zeros((part_rows, block), jnp.bfloat16)

            summed = partial[h, c, z_rows(z), :].astype(jnp.float32)
            for source in range(nz):
                summed = summed + arrived[h, c, source].astype(jnp.float32)
            sums.append(summed)
        at = slice(c * block, (c + 1) * block)
        block_scaled = gain_ref[:, at] * (jnp.concatenate(sums, axis=0) * (16.0 * factor))
        scaled.append(block_scaled)
        inner = inner + jnp.sum(block_scaled * hidden[:, at], axis=1, keepdims=True)
    inner = inverse_rms * inverse_rms * inverse_rms * inner / width
    hidden_grad = jnp.concatenate(
        [
            (inverse_rms * scaled[c] - hidden[:, c * block : (c + 1) * block] * inner).astype(
                jnp.bfloat16
            )
            for c in range(n_blocks)
        ],
        axis=1,
    )
    result = jnp.zeros((rows, width), jnp.float32)
    for m in range(n_mp):
        result = result + lax.dot_general(
            hidden_grad[:, m * part_width : (m + 1) * part_width], weights_in[m],
            (((1,), (1,)), ((), ())), preferred_element_type=jnp.float32,
        )
    grad_ref[...] = result.astype(jnp.bfloat16)
    for copy in sends:
        copy.wait_send()
    for condition, make in guarded:

        @pl.when(condition)
        def _(make=make):
            make().wait_send()


def finish_kernel(
    loss_in, grad_in, next_in, loss_ref, grad_ref, next_ref, sem_out
):
    count = next_in.shape[0] // 4
    stores = [pltpu.make_async_copy(grad_in, grad_ref, sem_out.at[4])]
    stores[0].start()
    for i in range(4):
        at = pl.ds(i * count, count)
        stores.append(pltpu.make_async_copy(next_in.at[at], next_ref.at[at], sem_out.at[i]))
        stores[-1].start()
    count = loss_ref.shape[1] // HALVES
    for h in range(HALVES):
        loss_ref[:, h * count : (h + 1) * count] = loss_in[h : h + 1, 0:count]
    for store in stores:
        store.wait()


def shards(n_queue, n_mp, speech, weight, norm_gain, queue_keys, new_keys, pointer, positives):
    rows, width = speech.shape
    key_count = queue_keys.shape[0]
    nz = n_queue // GROUP
    n_chunks = key_chunks(key_count // n_mp)
    vmem = pl.BlockSpec(memory_space=pltpu.VMEM)
    anywhere = pl.BlockSpec(memory_space=pl.ANY)
    dma = pltpu.SemaphoreType.DMA
    bf16, f32 = jnp.bfloat16, jnp.float32
    scratch = [
        pltpu.VMEM((rows, width), bf16),
        pltpu.VMEM(new_keys.shape, bf16),
        pltpu.VMEM((GROUP * key_count, width), bf16),
        pltpu.VMEM((n_mp, width, width // n_mp), bf16),
        pltpu.VMEM((HALVES, nz * rows // HALVES, width), bf16),
        pltpu.VMEM((nz, 8, LANES), jnp.int32),
        pltpu.VMEM((HALVES, nz * rows // HALVES, GROUP * key_count), f32),
        pltpu.VMEM((nz * rows // HALVES, GROUP * key_count), bf16),
        pltpu.VMEM((rows, width), f32),
        pltpu.VMEM((HALVES, width // 256, nz * rows // HALVES, 256), bf16),
        pltpu.VMEM((HALVES, width // 256, nz, rows // HALVES, 256), bf16),
        pltpu.VMEM((HALVES, width // 256, rows // HALVES, 256), bf16),
        pltpu.VMEM((HALVES, nz, nz, 8, LANES), f32),
        pltpu.VMEM((HALVES, nz * rows // HALVES, LANES), f32),
        pltpu.VMEM((HALVES, nz * rows // HALVES, LANES), f32),
        pltpu.VMEM((HALVES, nz * rows // HALVES, LANES), f32),
        pltpu.VMEM((HALVES, nz * rows // HALVES, LANES), jnp.int32),
        dma((4,)),
    ]
    scratch += [dma((n_mp, WEIGHT_CHUNKS))] * 10
    scratch += [dma((1,))] * 2 + [dma((n_chunks,))] * 2 + [dma((n_mp, n_chunks))] * 2
    scratch += [dma((n_chunks,))] * 2 + [dma((n_mp, n_chunks))] * 2
    scratch += [dma((HALVES, nz, nz)), dma((HALVES, nz))]
    scratch += [dma((nz,))] * 2 + [dma((HALVES, nz))] * 2
    scratch += [dma((HALVES, width // 256, nz))] * 2 + [dma((HALVES, width // 256))]
    loss, grad, queue_next = pl.pallas_call(
        functools.partial(step_kernel, n_queue, n_mp),
        out_shape=(
            pltpu.VMEM((8, LANES), f32),
            pltpu.VMEM((rows, width), bf16),
            pltpu.VMEM((key_count, width), bf16),
        ),
        in_specs=[anywhere, anywhere, vmem, anywhere, anywhere, pl.BlockSpec(memory_space=pltpu.SMEM), vmem],
        out_specs=(vmem, vmem, vmem),
        scratch_shapes=scratch,
        compiler_params=pltpu.CompilerParams(
            collective_id=0, has_side_effects=True, vmem_limit_bytes=248 * 256 * 1024
        ),
        name="contrast_step",
    )(speech, weight, norm_gain[None, :], queue_keys, new_keys, pointer, positives[None, :])
    loss, grad, queue_next = pl.pallas_call(
        finish_kernel,
        out_shape=(
            jax.ShapeDtypeStruct((1, rows), f32),
            jax.ShapeDtypeStruct((rows, width), bf16),
            jax.ShapeDtypeStruct((key_count, width), bf16),
        ),
        in_specs=[vmem, vmem, vmem],
        out_specs=(vmem, anywhere, anywhere),
        scratch_shapes=[
            dma((5,)),
        ],
        compiler_params=pltpu.CompilerParams(vmem_limit_bytes=16 * 1024 * 1024),
        name="hand_out",
    )(loss, grad, queue_next)
    return loss[0], grad, queue_next


def solution(mesh):
    n_queue, n_mp = mesh.shape["queue"], mesh.shape["mp"]
    return jax.shard_map(
        functools.partial(shards, n_queue, n_mp),
        mesh=mesh,
        in_specs=(
            P(("queue", "mp"), None),
            P(None, "mp"),
            P(),
            P("queue", None),
            P(),
            P(),
            P(("queue", "mp")),
        ),
        out_specs=(P(("queue", "mp")), P(("queue", "mp"), None), P("queue", None)),
        check_vma=False,
    )
```
